32 devices in a mesh: sample: 8 (over y, x, core), space: 4 (over z).
Axes of the slice: x: 2, y: 2, z: 4, core: 2. Of those that a mesh axis runs over, the one named last changes fastest.
Arguments:
- volumes: bfloat16 [32, 32, 2048], P('sample', None, 'space'), may hold values from -6 to 6
- grad_out: bfloat16 [32, 128, 256], P(('sample', 'space')), may hold values from -6 to 6
- kernel_first: bfloat16 [27, 64, 32], replicated, may hold values from -0.21875 to 0.21875
- bias_first: float32 [64], replicated, may hold values from -3 to 3
- kernel_second: bfloat16 [27, 128, 64], replicated, may hold values from -0.15625 to 0.15625
- bias_second: float32 [128], replicated, may hold values from -3 to 3
Outputs:
- features: bfloat16 [32, 128, 256], P(('sample', 'space'))
- kernel_grad_first: float32 [27, 64, 32], replicated
- bias_grad_first: float32 [64], replicated
- kernel_grad_second: float32 [27, 128, 64], replicated
- bias_grad_second: float32 [128], replicated
The draws below stay inside these ranges and needn't reach their ends.
All inputs are finite; a program needn't handle non-finite values.
Results may differ from the reference program's by a relative error of at most 0.0085.
The reference program's roundings to bfloat16 on the way (of `pooled`, `delta_two`, `spread` and `delta_one`) count: a program that leaves them out, or rounds other values in their place, can miss the bound.
Values may be sent and summed in bfloat16 or wider, within the bound.
No kernel may reach another device: no remote copies, remote signals or barrier semaphores. Data moves between devices by JAX's collectives and lax.ppermute only.
A program may use at most 192 MiB of HBM per device.

```python
import math
import jax
import jax.numpy as jnp
from jax import lax

C0 = 32
C1 = 64
C2 = 128
SIDE = 8
BATCH = 32
DEPTH = 32
DEPTH2 = 16
SIDE2 = 4


def levels(own_key, shape, split, low, high):
    def one(axis_at, parts):
        heights = jax.random.uniform(jax.random.fold_in(jax.random.fold_in(own_key, 6), axis_at), (parts,), jnp.float32, low / len(split), high / len(split))
        return jnp.repeat(jnp.exp(heights), shape[axis_at] // parts).reshape((-1,) + (1,) * (len(shape) - axis_at - 1))

    loudness = one(*split[0])
    for cut in split[1:]:
        loudness = loudness * one(*cut)
    return loudness


def scatter_about(rng, dims, width, reach, split=(), kind=jnp.bfloat16):
    values = jax.random.normal(rng, dims, jnp.float32) * width
    if len(split) > 0:
        values = levels(rng, dims, split, -0.22, 0.18) * values
    return jnp.clip(values, min=-reach, max=reach).astype(kind)


def setup_inputs(seed: int = 0) -> dict:
    seeds = jax.random.split(jax.random.key(seed), 7)
    volumes = scatter_about(seeds[0], (BATCH, C0, DEPTH * SIDE * SIDE), 1.0, 6.0, ((0, 8), (2, 4)))
    grad_out = scatter_about(seeds[1], (BATCH, C2, DEPTH2 * SIDE2 * SIDE2), 1.0, 6.0, ((0, 32),))
    kernel_first = scatter_about(seeds[2], (27, C1, C0), (27 * C0) ** -0.5, 0.21875)
    bias_first = scatter_about(seeds[3], (C1,), 0.5, 3.0, (), jnp.float32)
    kernel_second = scatter_about(seeds[4], (27, C2, C1), (27 * C1) ** -0.5, 0.15625)
    bias_second = scatter_about(seeds[5], (C2,), 0.5, 3.0, (), jnp.float32)
    return dict(volumes=volumes, grad_out=grad_out, kernel_first=kernel_first, bias_first=bias_first, kernel_second=kernel_second, bias_second=bias_second)


LEAK_SLOPE = 0.3

def leaky_unit(values):
    return jnp.where(values > 0, values, LEAK_SLOPE * values)

def leaky_slope(values):
    return jnp.where(values > 0, 1.0, LEAK_SLOPE).astype(values.dtype)

def pad_cube(flat, depth_len, side_len):
    cube_view = flat.reshape(flat.shape[0], flat.shape[1], depth_len, side_len, side_len)
    return jnp.pad(cube_view, ((0, 0), (0, 0), (1, 1), (1, 1), (1, 1)))

def tap_window(padded, tap_index, depth_len, side_len, mirror):
    deep_off = tap_index // 9
    high_off = tap_index // 3 % 3
    wide_off = tap_index % 3
    if mirror:
        deep_off, high_off, wide_off = (2 - deep_off, 2 - high_off, 2 - wide_off)
    window = padded[:, :, deep_off:deep_off + depth_len, high_off:high_off + side_len, wide_off:wide_off + side_len]
    return window.reshape(padded.shape[0], padded.shape[1], depth_len * side_len * side_len)

def convolve(padded, weight, depth_len, side_len):
    summed = jnp.zeros((padded.shape[0], weight.shape[1], depth_len * side_len * side_len), jnp.float32)
    for tap_index in range(27):
        window = tap_window(padded, tap_index, depth_len, side_len, False).astype(jnp.float32)
        summed = summed + jnp.einsum('oc,vcn->von', weight[tap_index].astype(jnp.float32), window)
    return summed

def weight_grad(gradient, padded, depth_len, side_len):
    rows = []
    for tap_index in range(27):
        window = tap_window(padded, tap_index, depth_len, side_len, False).astype(jnp.float32)
        rows.append(jnp.einsum('von,vcn->oc', gradient.astype(jnp.float32), window))
    return jnp.stack(rows)

def spread_back(delta, weight, depth_len, side_len):
    padded = pad_cube(delta, depth_len, side_len)
    summed = jnp.zeros((delta.shape[0], weight.shape[2], depth_len * side_len * side_len), jnp.float32)
    for tap_index in range(27):
        window = tap_window(padded, tap_index, depth_len, side_len, True).astype(jnp.float32)
        summed = summed + jnp.einsum('oc,von->vcn', weight[tap_index].astype(jnp.float32), window)
    return summed

def pool_mean(values, depth_len, side_len):
    lead_dim, chan_dim = (values.shape[0], values.shape[1])
    cube_view = values.reshape(lead_dim, chan_dim, depth_len // 2, 2, side_len // 2, 2, side_len // 2, 2)
    return lax.optimization_barrier(jnp.mean(cube_view, axis=(3, 5, 7))).reshape(lead_dim, chan_dim, -1)

def unpool_even(values, depth_len, side_len):
    lead_dim, chan_dim = (values.shape[0], values.shape[1])
    shape_small = (lead_dim, chan_dim, depth_len // 2, 1, side_len // 2, 1, side_len // 2, 1)
    shape_large = (lead_dim, chan_dim, depth_len // 2, 2, side_len // 2, 2, side_len // 2, 2)
    cube_view = jnp.broadcast_to(values.reshape(shape_small), shape_large)
    return cube_view.reshape(lead_dim, chan_dim, -1)

def reference(volumes, grad_out, kernel_first, bias_first, kernel_second, bias_second):

    def one_volume(running, scan_item):
        kernel_one, bias_one, kernel_two, bias_two = running
        volume, cotangent = scan_item
        volume = volume[None]
        cotangent = cotangent[None]
        padded_in = pad_cube(volume, DEPTH, SIDE)
        first_pre = convolve(padded_in, kernel_first, DEPTH, SIDE) + bias_first[None, :, None]
        pooled = pool_mean(leaky_unit(first_pre), DEPTH, SIDE).astype(jnp.bfloat16)
        padded_mid = pad_cube(pooled, DEPTH2, SIDE2)
        second = convolve(padded_mid, kernel_second, DEPTH2, SIDE2) + bias_second[None, :, None]
        features = leaky_unit(second).astype(jnp.bfloat16)
        delta_two = (cotangent.astype(jnp.float32) * leaky_slope(second)).astype(jnp.bfloat16)
        kernel_two = kernel_two + weight_grad(delta_two, padded_mid, DEPTH2, SIDE2)
        bias_two = bias_two + lax.optimization_barrier(jnp.sum(delta_two.astype(jnp.float32), axis=(0, 2)))
        spread = spread_back(delta_two, kernel_second, DEPTH2, SIDE2).astype(jnp.bfloat16)
        delta_one = (unpool_even(spread.astype(jnp.float32), DEPTH, SIDE) * 0.125 * leaky_slope(first_pre)).astype(jnp.bfloat16)
        kernel_one = kernel_one + weight_grad(delta_one, padded_in, DEPTH, SIDE)
        bias_one = bias_one + lax.optimization_barrier(jnp.sum(delta_one.astype(jnp.float32), axis=(0, 2)))
        return ((kernel_one, bias_one, kernel_two, bias_two), features[0])
    start = (jnp.zeros((27, C1, C0), jnp.float32), jnp.zeros((C1,), jnp.float32), jnp.zeros((27, C2, C1), jnp.float32), jnp.zeros((C2,), jnp.float32))
    running, features = lax.scan(one_volume, start, (volumes, grad_out))
    scale_one = 1.0 / math.sqrt(BATCH * DEPTH * SIDE * SIDE)
    scale_two = 1.0 / math.sqrt(BATCH * DEPTH2 * SIDE2 * SIDE2)
    return (features, running[0] * scale_one, running[1] * scale_one, running[2] * scale_two, running[3] * scale_two)
```

```python
import functools
import math

import jax
import jax.numpy as jnp
from jax import lax
from jax.experimental import pallas as pl
from jax.experimental.pallas import tpu as pltpu
from jax.sharding import PartitionSpec as P

SIDE = 8
LEAK_SLOPE = 0.3
LANES = 128
ROWS = 16
BF16 = jnp.bfloat16
F32 = jnp.float32


def vmem():
    return pl.BlockSpec(memory_space=pltpu.VMEM)


def lane_iota(rows):
    return lax.broadcasted_iota(jnp.int32, (rows, LANES), 1)


def turn(block, shift):
    return pltpu.roll(block, (-shift) % LANES, 1) if shift % LANES else block


def dot(left, right):
    return jnp.dot(left, right, preferred_element_type=F32)


def dot_lanes(left, right):
    return lax.dot_general(left, right, (((1,), (1,)), ((), ())), preferred_element_type=F32)


def in_plane(side, tap):
    high, wide = tap // 3 - 1, tap % 3 - 1
    lane = lane_iota(1)
    row, col = lane // side % side + high, lane % side + wide
    valid = (row >= 0) & (row < side) & (col >= 0) & (col < side)
    return valid, high * side + wide


def weights_kernel(first_ref, second_ref, bias_one_ref, bias_two_ref, conv_one_ref, conv_two_ref, back_ref, col_one_ref, col_two_ref):
    mid, out = first_ref.shape[2], second_ref.shape[2]
    inner, deep = first_ref.shape[1], second_ref.shape[1]

    def eye(size):
        row = lax.broadcasted_iota(jnp.int32, (size, size), 0)
        return row == lax.broadcasted_iota(jnp.int32, (size, size), 1)

    for a in range(3):
        taps = first_ref[9 * a : 9 * a + 9].reshape(9 * inner, mid)
        conv_one_ref[a * mid : (a + 1) * mid, :] = dot_lanes(eye(mid).astype(BF16), taps).astype(BF16)
        taps = second_ref[9 * a : 9 * a + 9].reshape(9 * deep, out)
        conv_two_ref[a * out : (a + 1) * out, :] = dot_lanes(eye(out).astype(BF16), taps).astype(BF16)
        for t in range(9):
            back_ref[a * deep : (a + 1) * deep, t * out : (t + 1) * out] = second_ref[9 * a + t]
    for row_ref, col_ref, size in ((bias_one_ref, col_one_ref, mid), (bias_two_ref, col_two_ref, out)):
        col = jnp.sum(jnp.where(eye(size), row_ref[...], 0.0), axis=1, keepdims=True)
        col_ref[...] = jnp.broadcast_to(col, (size, LANES))


def prepare_weights(kernel_first, bias_first, kernel_second, bias_second):
    first, second = jnp.swapaxes(kernel_first, 1, 2), jnp.swapaxes(kernel_second, 1, 2)
    inner, mid, out = first.shape[1], first.shape[2], second.shape[2]
    shapes = (
        ((3 * mid, 9 * inner), BF16),
        ((3 * out, 9 * mid), BF16),
        ((3 * mid, 9 * out), BF16),
        ((mid, LANES), F32),
        ((out, LANES), F32),
    )
    return pl.pallas_call(
        weights_kernel,
        out_shape=[jax.ShapeDtypeStruct(s, d) for s, d in shapes],
        in_specs=[vmem()] * 4,
        out_specs=[vmem()] * 5,
        name="weights",
    )(first, second, bias_first.reshape(1, -1), bias_second.reshape(1, -1))


def main_kernel(plan, *refs):
    parts, grad_ref, conv_one_ref, conv_two_ref, back_ref, col_one_ref, col_two_ref = (
        refs[: plan.space],
        *refs[plan.space : plan.space + 6],
    )
    feat_ref, keep_ref, send_ref = refs[plan.space + 6 : plan.space + 9]
    x_ref, s_one, t_one, slope_ref, lk_ref, d_one, s_two, t_two, d_two, sd_two, u_two, pay_ref = refs[plan.space + 9 :]
    inner, mid, out = plan.inner, plan.mid, plan.out
    blocks, halves = plan.blocks, plan.halves
    place, core = lax.axis_index("space"), lax.axis_index("sample") % plan.cores
    side, small = SIDE, SIDE // 2
    plane = side * side
    low = small * small
    lane = lane_iota(1)

    s_one[9 * inner :, :] = jnp.ones((ROWS, blocks * LANES), BF16)
    s_two[9 * mid :, :] = jnp.ones((ROWS, halves * LANES), BF16)
    cell = lax.broadcasted_iota(jnp.int32, (LANES, LANES), 0)
    lanes = lax.broadcasted_iota(jnp.int32, (LANES, LANES), 1)
    parent = (cell % plane // side // 2) * small + cell % side // 2
    pool = jnp.where(parent == lanes % low, 0.125, 0.0).astype(BF16)
    pool = jnp.concatenate([pool, pool], axis=0)
    parent = (lanes % plane // side // 2) * small + lanes % side // 2

    for volume in range(plan.owned):
        for k, part in enumerate(parts):
            start = (place ^ k) * plan.part_blocks
            for j in range(plan.part_blocks):
                x_ref[start + j] = part[volume, :, j * LANES : (j + 1) * LANES]

        for tap in range(9):
            valid, shift = in_plane(side, tap)
            for j in range(blocks):
                block = x_ref[j]
                if shift:
                    block = jnp.where(valid, turn(block, shift), jnp.zeros_like(block))
                s_one[tap * inner : (tap + 1) * inner, j * LANES : (j + 1) * LANES] = block

        t_one[...] = dot(conv_one_ref[...], s_one[: 9 * inner, :])

        upper = lane >= plane
        for j in range(blocks):
            here = slice(j * LANES, (j + 1) * LANES)
            before, after = slice(here.start - LANES, here.start), slice(here.stop, here.stop + LANES)
            zero = jnp.zeros((mid, LANES), F32)
            up = jnp.where(upper, t_one[:mid, before] if j else zero, t_one[:mid, here])
            down = jnp.where(upper, t_one[2 * mid :, here], t_one[2 * mid :, after] if j < blocks - 1 else zero)
            pre = t_one[mid : 2 * mid, here] + turn(up + down, plane) + col_one_ref[...]
            slope = jnp.where(pre > 0, 1.0, LEAK_SLOPE)
            slope_ref[:, here] = slope * 0.125
            value = slope * pre
            high = value.astype(BF16)
            lk_ref[j * mid : (j + 1) * mid, :LANES] = high
            lk_ref[j * mid : (j + 1) * mid, LANES:] = (value - high.astype(F32)).astype(BF16)

        means = dot(lk_ref[...], pool)
        for h in range(halves):
            here = slice(h * LANES, (h + 1) * LANES)
            pooled = jnp.zeros((mid, LANES), F32)
            for j in range(LANES // low):
                row = (h * (LANES // low) + j) * mid
                pooled = jnp.where(lane // low == j, means[row : row + mid], pooled)
            for tap in range(9):
                valid, shift = in_plane(small, tap)
                block = jnp.where(valid, turn(pooled, shift), 0.0) if shift else pooled
                s_two[tap * mid : (tap + 1) * mid, here] = block.astype(BF16)

        t_two[...] = dot(conv_two_ref[...], s_two[: 9 * mid, :])
        deltas = []
        for h in range(halves):
            here = slice(h * LANES, (h + 1) * LANES)
            before, after = slice(here.start - LANES, here.start), slice(here.stop, here.stop + LANES)
            zero = jnp.zeros((out, LANES), F32)
            up = jnp.where(lane >= LANES - low, t_two[:out, before] if h else zero, t_two[:out, here])
            down = jnp.where(lane < low, t_two[2 * out :, after] if h < halves - 1 else zero, t_two[2 * out :, here])
            pre = t_two[out : 2 * out, here] + turn(up, -low) + turn(down, low) + col_two_ref[...]
            slope = jnp.where(pre > 0, 1.0, LEAK_SLOPE)
            feat_ref[volume, :, here] = (slope * pre).astype(BF16)
            delta = (grad_ref[volume, :, here].astype(F32) * slope).astype(BF16).astype(F32)
            deltas.append(delta)
            for tap in range(9):
                valid, shift = in_plane(small, 8 - tap)
                block = jnp.where(valid, turn(delta, shift), 0.0) if shift else delta
                sd_two[tap * out : (tap + 1) * out, here] = block.astype(BF16)

        for h in range(halves):
            here = slice(h * LANES, (h + 1) * LANES)
            zero = jnp.zeros((out, LANES), F32)
            after = deltas[h + 1] if h < halves - 1 else zero
            before = deltas[h - 1] if h else zero
            d_two[:out, here] = turn(jnp.where(lane < low, after, deltas[h]), low).astype(BF16)
            d_two[out : 2 * out, here] = deltas[h].astype(BF16)
            d_two[2 * out :, here] = turn(jnp.where(lane >= LANES - low, before, deltas[h]), -low).astype(BF16)

        u_two[...] = dot(back_ref[...], sd_two[...])
        spreads = []
        for h in range(halves):
            here = slice(h * LANES, (h + 1) * LANES)
            before, after = slice(here.start - LANES, here.start), slice(here.stop, here.stop + LANES)
            zero = jnp.zeros((mid, LANES), F32)
            down = jnp.where(lane < low, u_two[:mid, after] if h < halves - 1 else zero, u_two[:mid, here])
            up = jnp.where(lane >= LANES - low, u_two[2 * mid :, before] if h else zero, u_two[2 * mid :, here])
            spreads.append((u_two[mid : 2 * mid, here] + turn(down, low) + turn(up, -low)).astype(BF16))
        spread = jnp.concatenate(spreads, axis=0)

        deltas = []
        for j in range(LANES // low):
            unpool = jnp.where(parent + j * low == cell, 1.0, 0.0).astype(BF16)
            deltas.append(dot(spread, unpool))
        wide = []
        for j in range(blocks):
            here = slice(j * LANES, (j + 1) * LANES)
            h, i = j // (LANES // low), j % (LANES // low)
            wide.append(deltas[i][h * mid : (h + 1) * mid] * slope_ref[:, here])
        for j in range(blocks):
            here = slice(j * LANES, (j + 1) * LANES)
            zero = jnp.zeros((mid, LANES), F32)
            after = wide[j + 1] if j < blocks - 1 else zero
            before = wide[j - 1] if j else zero
            d_one[:mid, here] = turn(jnp.where(upper, wide[j], after), plane).astype(BF16)
            d_one[mid : 2 * mid, here] = wide[j].astype(BF16)
            d_one[2 * mid :, here] = turn(jnp.where(upper, before, wide[j]), plane).astype(BF16)

        two = dot_lanes(s_two[...], d_two[...]) * plan.scale_two
        one = dot_lanes(s_one[...], d_one[...]) * plan.scale_one
        first = 9 * inner
        total = 27 * mid
        half = first // 2
        pieces = [(a * 9 * mid, two[: 9 * mid, a * out : (a + 1) * out]) for a in range(3)]
        pieces.append((total, one[:first, : 2 * mid]))
        pieces.append((total + first, jnp.concatenate([one[:half, 2 * mid :], one[half:first, 2 * mid :]], axis=1)))
        row = lax.broadcasted_iota(jnp.int32, (ROWS // 2, LANES), 0)
        own = one[first : first + ROWS // 2, : 2 * mid]
        own = jnp.where(lane_iota(1) < mid, turn(own, mid), 0.0)
        tail = jnp.where(row == 0, two[9 * mid : 9 * mid + ROWS // 2, out : 2 * out], jnp.where(row == 1, own, 0.0))
        if volume:
            tail = tail + pay_ref[plan.total - ROWS : plan.total - ROWS // 2] + pay_ref[plan.total - ROWS // 2 :]
        for start, piece in pieces:
            span = slice(start, start + piece.shape[0])
            pay_ref[span, :] = piece + pay_ref[span, :] if volume else piece
        used = total + first + half
        if not volume and used < plan.total - ROWS:
            pay_ref[used : plan.total - ROWS, :] = jnp.zeros((plan.total - ROWS - used, LANES), F32)
        high = tail.astype(BF16).astype(F32)
        pay_ref[plan.total - ROWS :, :] = jnp.concatenate([high, tail - high], axis=0)

    share = plan.total // plan.cores
    keep_ref[...] = pay_ref[pl.ds(pl.multiple_of(core * share, ROWS), share), :]
    send_ref[...] = pay_ref[pl.ds(pl.multiple_of((1 - core) * share, ROWS), share), :].astype(BF16)


def split_again(values, plan, last):
    rows = values.shape[0]
    tail = values[rows - ROWS : rows - ROWS // 2] + values[rows - ROWS // 2 :]
    high = tail.astype(BF16).astype(F32)
    parted = jnp.concatenate([high, tail - high], axis=0)
    return jnp.where(last, parted, values[rows - ROWS :])


def core_sum_kernel(plan, keep_ref, got_ref, own_ref, *rest):
    sends, sum_ref = rest[:-1], rest[-1]
    group = lax.axis_index("sample") // plan.cores
    core = lax.axis_index("sample") % plan.cores
    rows = keep_ref.shape[0]
    sum_ref[...] = keep_ref[...] + got_ref[...].astype(F32)
    sum_ref[rows - ROWS :, :] = split_again(sum_ref[rows - ROWS :, :], plan, core == plan.cores - 1)

    def chunk(k):
        return sum_ref[pl.ds(pl.multiple_of((group ^ k) * plan.chunk, ROWS), plan.chunk), :]

    own_ref[...] = chunk(0)
    for k, send in enumerate(sends, start=1):
        send[...] = chunk(k).astype(BF16)


def last_chunk(plan):
    return lax.axis_index("sample") == lax.axis_size("sample") - 1


def group_sum_kernel(plan, own_ref, *rest):
    gots, out_ref = rest[:-1], rest[-1]
    total = own_ref[...]
    for got in gots:
        total = total + got[...].astype(F32)
    rows = total.shape[0]
    out_ref[: rows - ROWS, :] = total[: rows - ROWS].astype(BF16)
    out_ref[rows - ROWS :, :] = split_again(total[rows - ROWS :], plan, last_chunk(plan)).astype(BF16)


def space_sum_kernel(plan, *refs):
    values, out_ref = [ref[...].astype(F32) for ref in refs[:-1]], refs[-1]
    while len(values) > 1:
        values = [values[i] + values[i + 1] for i in range(0, len(values), 2)]
    total = values[0]
    rows = total.shape[0]
    out_ref[: rows - ROWS, :] = total[: rows - ROWS].astype(BF16)
    out_ref[rows - ROWS :, :] = split_again(total[rows - ROWS :], plan, last_chunk(plan)).astype(BF16)


def gather_kernel(plan, *refs):
    chunks, out_ref = refs[:-1], refs[-1]
    group = lax.axis_index("sample") // plan.cores
    for k, ref in enumerate(chunks):
        out_ref[pl.ds(pl.multiple_of((group ^ k) * plan.chunk, ROWS), plan.chunk), :] = ref[...]


def unpack_kernel(plan, mine_ref, other_ref, one_ref, bias_one_ref, two_ref, bias_two_ref, all_ref):
    inner, mid, out = plan.inner, plan.mid, plan.out
    core = lax.axis_index("sample") % plan.cores
    share = plan.total // plan.cores
    all_ref[pl.ds(pl.multiple_of(core * share, ROWS), share), :] = mine_ref[...].astype(F32)
    all_ref[pl.ds(pl.multiple_of((1 - core) * share, ROWS), share), :] = other_ref[...].astype(F32)
    total, first = 27 * mid, 9 * inner
    two_ref[...] = all_ref[:total, :].reshape(27, mid, out)
    pair = all_ref[total : total + first, :]
    one_ref[0:9] = pair[:, :mid].reshape(9, inner, mid)
    one_ref[9:18] = pair[:, mid:].reshape(9, inner, mid)
    pair = all_ref[total + first : total + first + first // 2, :]
    pair = jnp.concatenate([pair[:, :mid], pair[:, mid:]], axis=0)
    one_ref[18:27] = pair.reshape(9, inner, mid)
    tail = all_ref[plan.total - ROWS : plan.total - ROWS // 2, :] + all_ref[plan.total - ROWS // 2 : plan.total, :]
    bias_two_ref[...] = tail[0:1, :out]
    bias_one_ref[...] = tail[1:2, :mid]


class Plan:
    def __init__(self, volumes, kernel_first, kernel_second):
        self.space, self.sample = lax.axis_size("space"), lax.axis_size("sample")
        self.inner, self.mid, self.out = kernel_first.shape[2], kernel_first.shape[1], kernel_second.shape[1]
        self.owned = volumes.shape[0] // self.space
        self.part_blocks = volumes.shape[2] // LANES
        self.blocks = self.part_blocks * self.space
        self.halves = self.blocks // 8
        self.cores = 2
        self.groups = self.sample // self.cores
        cells = self.blocks * LANES * volumes.shape[0] * self.sample
        self.scale_one = 1.0 / math.sqrt(cells)
        self.scale_two = 1.0 / math.sqrt(cells // 8)
        used = 27 * self.mid + 9 * self.inner * 3 // 2 + ROWS
        step = ROWS * self.groups * self.cores
        self.total = -(-used // step) * step
        self.chunk = self.total // self.groups // self.cores


def call(kernel, plan, name, out_shapes, *args, scratch=(), limit=None):
    return pl.pallas_call(
        functools.partial(kernel, plan),
        out_shape=[jax.ShapeDtypeStruct(s, d) for s, d in out_shapes],
        in_specs=[vmem()] * len(args),
        out_specs=[vmem()] * len(out_shapes),
        scratch_shapes=[pltpu.VMEM(s, d) for s, d in scratch],
        compiler_params=pltpu.CompilerParams(vmem_limit_bytes=limit),
        name=name,
    )(*args)


def swap(value, axis, k):
    return lax.ppermute(value, axis, [(i, i ^ k) for i in range(lax.axis_size(axis))])


def on_device(volumes, grad_out, kernel_first, bias_first, kernel_second, bias_second):
    plan = Plan(volumes, kernel_first, kernel_second)
    inner, mid, out = plan.inner, plan.mid, plan.out
    me = lax.axis_index("space")

    def piece(k):
        return lax.dynamic_slice_in_dim(volumes, (me ^ k) * plan.owned, plan.owned, axis=0)

    parts = [piece(0)] + [swap(piece(k), "space", k) for k in range(1, plan.space)]
    weights = prepare_weights(kernel_first, bias_first, kernel_second, bias_second)
    cells, small = plan.blocks * LANES, plan.halves * LANES
    share = plan.total // plan.cores
    scratch = (
        ((plan.blocks, inner, LANES), BF16),
        ((9 * inner + ROWS, cells), BF16),
        ((3 * mid, cells), F32),
        ((mid, cells), F32),
        ((plan.blocks * mid, 2 * LANES), BF16),
        ((3 * mid, cells), BF16),
        ((9 * mid + ROWS, small), BF16),
        ((3 * out, small), F32),
        ((3 * out, small), BF16),
        ((9 * out, small), BF16),
        ((3 * mid, small), F32),
        ((plan.total, LANES), F32),
    )
    features, keep, send = call(
        main_kernel,
        plan,
        "main",
        (((plan.owned, out, small), BF16), ((share, LANES), F32), ((share, LANES), BF16)),
        *parts,
        grad_out,
        *weights,
        scratch=scratch,
        limit=48 * 1024 * 1024,
    )
    chunk = (plan.chunk, LANES)
    got = swap(send, "sample", 1)
    own, *sends = call(core_sum_kernel, plan, "core_sum", ((chunk, F32),) + ((chunk, BF16),) * (plan.groups - 1), keep, got, scratch=(((share, LANES), F32),))
    gots = [swap(s, "sample", plan.cores * k) for k, s in enumerate(sends, start=1)]
    (partial,) = call(group_sum_kernel, plan, "group_sum", ((chunk, BF16),), own, *gots)
    gots = [swap(partial, "space", k) for k in range(1, plan.space)]
    (whole,) = call(space_sum_kernel, plan, "space_sum", ((chunk, BF16),), partial, *gots)
    gots = [swap(whole, "sample", plan.cores * k) for k in range(1, plan.groups)]
    (mine,) = call(gather_kernel, plan, "gather", (((share, LANES), BF16),), whole, *gots)
    other = swap(mine, "sample", 1)
    one, bias_one, two, bias_two = call(
        unpack_kernel,
        plan,
        "unpack",
        (((27, inner, mid), F32), ((1, mid), F32), ((27, mid, out), F32), ((1, out), F32)),
        mine,
        other,
        scratch=(((plan.total, LANES), F32),),
    )
    return (features, jnp.swapaxes(one, 1, 2), bias_one.reshape(mid), jnp.swapaxes(two, 1, 2), bias_two.reshape(out))


def solution(mesh):
    in_specs = (P("sample", None, "space"), P(("sample", "space"), None, None), P(), P(), P(), P())
    out_specs = (P(("sample", "space"), None, None), P(), P(), P(), P())
    return jax.shard_map(
        on_device, mesh=mesh, in_specs=in_specs, out_specs=out_specs, check_vma=False
    )
```

```python
import functools
import math

import jax
import jax.numpy as jnp
from jax import lax
from jax.experimental import pallas as pl
from jax.experimental.pallas import tpu as pltpu
from jax.sharding import PartitionSpec as P

SIDE = 8
LEAK_SLOPE = 0.3
LANES = 128
ROWS = 16
SMALL_LIMIT = 4 * 1024 * 1024
BF16 = jnp.bfloat16
F32 = jnp.float32


def vmem():
    return pl.BlockSpec(memory_space=pltpu.VMEM)


def lane_iota(rows):
    return lax.broadcasted_iota(jnp.int32, (rows, LANES), 1)


def turn(block, shift):
    return pltpu.roll(block, (-shift) % LANES, 1) if shift % LANES else block


def dot(left, right):
    return jnp.dot(left, right, preferred_element_type=F32)


def dot_lanes(left, right):
    return lax.dot_general(left, right, (((1,), (1,)), ((), ())), preferred_element_type=F32)


def in_plane(side, tap):
    high, wide = tap // 3 - 1, tap % 3 - 1
    lane = lane_iota(1)
    row, col = lane // side % side + high, lane % side + wide
    valid = (row >= 0) & (row < side) & (col >= 0) & (col < side)
    return valid, high * side + wide


def weights_kernel(first_ref, second_ref, bias_one_ref, bias_two_ref, conv_one_ref, conv_two_ref, back_ref, col_one_ref, col_two_ref):
    mid, out = first_ref.shape[2], second_ref.shape[2]
    inner, deep = first_ref.shape[1], second_ref.shape[1]

    def eye(size):
        row = lax.broadcasted_iota(jnp.int32, (size, size), 0)
        return row == lax.broadcasted_iota(jnp.int32, (size, size), 1)

    for a in range(3):
        taps = first_ref[9 * a : 9 * a + 9].reshape(9 * inner, mid)
        conv_one_ref[a * mid : (a + 1) * mid, :] = dot_lanes(eye(mid).astype(BF16), taps).astype(BF16)
        taps = second_ref[9 * a : 9 * a + 9].reshape(9 * deep, out)
        conv_two_ref[a * out : (a + 1) * out, :] = dot_lanes(eye(out).astype(BF16), taps).astype(BF16)
        for t in range(9):
            back_ref[a * deep : (a + 1) * deep, t * out : (t + 1) * out] = second_ref[9 * a + t]
    for row_ref, col_ref, size in ((bias_one_ref, col_one_ref, mid), (bias_two_ref, col_two_ref, out)):
        col = jnp.sum(jnp.where(eye(size), row_ref[...], 0.0), axis=1, keepdims=True)
        col_ref[...] = jnp.broadcast_to(col, (size, LANES))


def prepare_weights(kernel_first, bias_first, kernel_second, bias_second):
    first, second = jnp.swapaxes(kernel_first, 1, 2), jnp.swapaxes(kernel_second, 1, 2)
    inner, mid, out = first.shape[1], first.shape[2], second.shape[2]
    shapes = (
        ((3 * mid, 9 * inner), BF16),
        ((3 * out, 9 * mid), BF16),
        ((3 * mid, 9 * out), BF16),
        ((mid, LANES), F32),
        ((out, LANES), F32),
    )
    return pl.pallas_call(
        weights_kernel,
        out_shape=[jax.ShapeDtypeStruct(s, d) for s, d in shapes],
        in_specs=[vmem()] * 4,
        out_specs=[vmem()] * 5,
        compiler_params=pltpu.CompilerParams(vmem_limit_bytes=SMALL_LIMIT),
        name="weights",
    )(first, second, bias_first.reshape(1, -1), bias_second.reshape(1, -1))


def main_kernel(plan, *refs):
    parts, grad_ref, conv_one_ref, conv_two_ref, back_ref, col_one_ref, col_two_ref = (
        refs[: plan.space],
        *refs[plan.space : plan.space + 6],
    )
    feat_ref, keep_ref, send_ref = refs[plan.space + 6 : plan.space + 9]
    x_ref, s_one, t_one, slope_ref, lk_ref, d_one, s_two, t_two, d_two, sd_two, u_two, pay_ref = refs[plan.space + 9 :]
    inner, mid, out = plan.inner, plan.mid, plan.out
    blocks, halves = plan.blocks, plan.halves
    place, core = lax.axis_index("space"), lax.axis_index("sample") % plan.cores
    side, small = SIDE, SIDE // 2
    plane = side * side
    low = small * small
    lane = lane_iota(1)

    s_one[9 * inner :, :] = jnp.ones((ROWS, blocks * LANES), BF16)
    s_two[9 * mid :, :] = jnp.ones((ROWS, halves * LANES), BF16)
    cell = lax.broadcasted_iota(jnp.int32, (LANES, LANES), 0)
    lanes = lax.broadcasted_iota(jnp.int32, (LANES, LANES), 1)
    parent = (cell % plane // side // 2) * small + cell % side // 2
    pool = jnp.where(parent == lanes % low, 0.125, 0.0).astype(BF16)
    pool = jnp.concatenate([pool, pool], axis=0)
    parent = (lanes % plane // side // 2) * small + lanes % side // 2

    for volume in range(plan.owned):
        for k, part in enumerate(parts):
            start = (place ^ k) * plan.part_blocks
            for j in range(plan.part_blocks):
                x_ref[start + j] = part[volume, :, j * LANES : (j + 1) * LANES]

        for tap in range(9):
            valid, shift = in_plane(side, tap)
            for j in range(blocks):
                block = x_ref[j]
                if shift:
                    block = jnp.where(valid, turn(block, shift), jnp.zeros_like(block))
                s_one[tap * inner : (tap + 1) * inner, j * LANES : (j + 1) * LANES] = block

        t_one[...] = dot(conv_one_ref[...], s_one[: 9 * inner, :])

        upper = lane >= plane
        for j in range(blocks):
            here = slice(j * LANES, (j + 1) * LANES)
            before, after = slice(here.start - LANES, here.start), slice(here.stop, here.stop + LANES)
            zero = jnp.zeros((mid, LANES), F32)
            up = jnp.where(upper, t_one[:mid, before] if j else zero, t_one[:mid, here])
            down = jnp.where(upper, t_one[2 * mid :, here], t_one[2 * mid :, after] if j < blocks - 1 else zero)
            pre = t_one[mid : 2 * mid, here] + turn(up + down, plane) + col_one_ref[...]
            slope = jnp.where(pre > 0, 1.0, LEAK_SLOPE)
            slope_ref[:, here] = slope * 0.125
            value = slope * pre
            high = value.astype(BF16)
            lk_ref[j * mid : (j + 1) * mid, :LANES] = high
            lk_ref[j * mid : (j + 1) * mid, LANES:] = (value - high.astype(F32)).astype(BF16)

        means = dot(lk_ref[...], pool)
        for h in range(halves):
            here = slice(h * LANES, (h + 1) * LANES)
            pooled = jnp.zeros((mid, LANES), F32)
            for j in range(LANES // low):
                row = (h * (LANES // low) + j) * mid
                pooled = jnp.where(lane // low == j, means[row : row + mid], pooled)
            for tap in range(9):
                valid, shift = in_plane(small, tap)
                block = jnp.where(valid, turn(pooled, shift), 0.0) if shift else pooled
                s_two[tap * mid : (tap + 1) * mid, here] = block.astype(BF16)

        t_two[...] = dot(conv_two_ref[...], s_two[: 9 * mid, :])
        deltas = []
        for h in range(halves):
            here = slice(h * LANES, (h + 1) * LANES)
            before, after = slice(here.start - LANES, here.start), slice(here.stop, here.stop + LANES)
            zero = jnp.zeros((out, LANES), F32)
            up = jnp.where(lane >= LANES - low, t_two[:out, before] if h else zero, t_two[:out, here])
            down = jnp.where(lane < low, t_two[2 * out :, after] if h < halves - 1 else zero, t_two[2 * out :, here])
            pre = t_two[out : 2 * out, here] + turn(up, -low) + turn(down, low) + col_two_ref[...]
            slope = jnp.where(pre > 0, 1.0, LEAK_SLOPE)
            feat_ref[volume, :, here] = (slope * pre).astype(BF16)
            delta = (grad_ref[volume, :, here].astype(F32) * slope).astype(BF16).astype(F32)
            deltas.append(delta)
            for tap in range(9):
                valid, shift = in_plane(small, 8 - tap)
                block = jnp.where(valid, turn(delta, shift), 0.0) if shift else delta
                sd_two[tap * out : (tap + 1) * out, here] = block.astype(BF16)

        for h in range(halves):
            here = slice(h * LANES, (h + 1) * LANES)
            zero = jnp.zeros((out, LANES), F32)
            after = deltas[h + 1] if h < halves - 1 else zero
            before = deltas[h - 1] if h else zero
            d_two[:out, here] = turn(jnp.where(lane < low, after, deltas[h]), low).astype(BF16)
            d_two[out : 2 * out, here] = deltas[h].astype(BF16)
            d_two[2 * out :, here] = turn(jnp.where(lane >= LANES - low, before, deltas[h]), -low).astype(BF16)

        u_two[...] = dot(back_ref[...], sd_two[...])
        spreads = []
        for h in range(halves):
            here = slice(h * LANES, (h + 1) * LANES)
            before, after = slice(here.start - LANES, here.start), slice(here.stop, here.stop + LANES)
            zero = jnp.zeros((mid, LANES), F32)
            down = jnp.where(lane < low, u_two[:mid, after] if h < halves - 1 else zero, u_two[:mid, here])
            up = jnp.where(lane >= LANES - low, u_two[2 * mid :, before] if h else zero, u_two[2 * mid :, here])
            spreads.append((u_two[mid : 2 * mid, here] + turn(down, low) + turn(up, -low)).astype(BF16))
        spread = jnp.concatenate(spreads, axis=0)

        deltas = []
        for j in range(LANES // low):
            unpool = jnp.where(parent + j * low == cell, 1.0, 0.0).astype(BF16)
            deltas.append(dot(spread, unpool))
        wide = []
        for j in range(blocks):
            here = slice(j * LANES, (j + 1) * LANES)
            h, i = j // (LANES // low), j % (LANES // low)
            wide.append(deltas[i][h * mid : (h + 1) * mid] * slope_ref[:, here])
        for j in range(blocks):
            here = slice(j * LANES, (j + 1) * LANES)
            zero = jnp.zeros((mid, LANES), F32)
            after = wide[j + 1] if j < blocks - 1 else zero
            before = wide[j - 1] if j else zero
            d_one[:mid, here] = turn(jnp.where(upper, wide[j], after), plane).astype(BF16)
            d_one[mid : 2 * mid, here] = wide[j].astype(BF16)
            d_one[2 * mid :, here] = turn(jnp.where(upper, before, wide[j]), plane).astype(BF16)

        two = dot_lanes(s_two[...], d_two[...]) * plan.scale_two
        one = dot_lanes(s_one[...], d_one[...]) * plan.scale_one
        first = 9 * inner
        total = 27 * mid
        half = first // 2
        pieces = [(a * 9 * mid, two[: 9 * mid, a * out : (a + 1) * out]) for a in range(3)]
        pieces.append((total, one[:first, : 2 * mid]))
        pieces.append((total + first, jnp.concatenate([one[:half, 2 * mid :], one[half:first, 2 * mid :]], axis=1)))
        row = lax.broadcasted_iota(jnp.int32, (ROWS // 2, LANES), 0)
        own = one[first : first + ROWS // 2, : 2 * mid]
        own = jnp.where(lane_iota(1) < mid, turn(own, mid), 0.0)
        tail = jnp.where(row == 0, two[9 * mid : 9 * mid + ROWS // 2, out : 2 * out], jnp.where(row == 1, own, 0.0))
        if volume:
            tail = tail + pay_ref[plan.total - ROWS : plan.total - ROWS // 2] + pay_ref[plan.total - ROWS // 2 :]
        for start, piece in pieces:
            span = slice(start, start + piece.shape[0])
            pay_ref[span, :] = piece + pay_ref[span, :] if volume else piece
        used = total + first + half
        if not volume and used < plan.total - ROWS:
            pay_ref[used : plan.total - ROWS, :] = jnp.zeros((plan.total - ROWS - used, LANES), F32)
        high = tail.astype(BF16).astype(F32)
        pay_ref[plan.total - ROWS :, :] = jnp.concatenate([high, tail - high], axis=0)

    share = plan.total // plan.cores
    keep_ref[...] = pay_ref[pl.ds(pl.multiple_of(core * share, ROWS), share), :]
    send_ref[...] = pay_ref[pl.ds(pl.multiple_of((1 - core) * share, ROWS), share), :].astype(BF16)


def split_again(values, plan, last):
    rows = values.shape[0]
    tail = values[rows - ROWS : rows - ROWS // 2] + values[rows - ROWS // 2 :]
    high = tail.astype(BF16).astype(F32)
    parted = jnp.concatenate([high, tail - high], axis=0)
    return jnp.where(last, parted, values[rows - ROWS :])


def core_sum_kernel(plan, keep_ref, got_ref, own_ref, *rest):
    sends, sum_ref = rest[:-1], rest[-1]
    group = lax.axis_index("sample") // plan.cores
    core = lax.axis_index("sample") % plan.cores
    rows = keep_ref.shape[0]
    sum_ref[...] = keep_ref[...] + got_ref[...].astype(F32)
    sum_ref[rows - ROWS :, :] = split_again(sum_ref[rows - ROWS :, :], plan, core == plan.cores - 1)

    def chunk(k):
        return sum_ref[pl.ds(pl.multiple_of((group ^ k) * plan.chunk, ROWS), plan.chunk), :]

    own_ref[...] = chunk(0)
    for k, send in enumerate(sends, start=1):
        send[...] = chunk(k).astype(BF16)


def last_chunk(plan):
    return lax.axis_index("sample") == lax.axis_size("sample") - 1


def group_sum_kernel(plan, own_ref, *rest):
    gots, out_ref = rest[:-1], rest[-1]
    total = own_ref[...]
    for got in gots:
        total = total + got[...].astype(F32)
    rows = total.shape[0]
    out_ref[: rows - ROWS, :] = total[: rows - ROWS].astype(BF16)
    out_ref[rows - ROWS :, :] = split_again(total[rows - ROWS :], plan, last_chunk(plan)).astype(BF16)


def space_sum_kernel(plan, *refs):
    values, out_ref = [ref[...].astype(F32) for ref in refs[:-1]], refs[-1]
    while len(values) > 1:
        values = [values[i] + values[i + 1] for i in range(0, len(values), 2)]
    total = values[0]
    rows = total.shape[0]
    out_ref[: rows - ROWS, :] = total[: rows - ROWS].astype(BF16)
    out_ref[rows - ROWS :, :] = split_again(total[rows - ROWS :], plan, last_chunk(plan)).astype(BF16)


def gather_kernel(plan, *refs):
    chunks, out_ref = refs[:-1], refs[-1]
    group = lax.axis_index("sample") // plan.cores
    for k, ref in enumerate(chunks):
        out_ref[pl.ds(pl.multiple_of((group ^ k) * plan.chunk, ROWS), plan.chunk), :] = ref[...]


def unpack_kernel(plan, mine_ref, other_ref, one_ref, bias_one_ref, two_ref, bias_two_ref, all_ref):
    inner, mid, out = plan.inner, plan.mid, plan.out
    core = lax.axis_index("sample") % plan.cores
    share = plan.total // plan.cores
    all_ref[pl.ds(pl.multiple_of(core * share, ROWS), share), :] = mine_ref[...].astype(F32)
    all_ref[pl.ds(pl.multiple_of((1 - core) * share, ROWS), share), :] = other_ref[...].astype(F32)
    total, first = 27 * mid, 9 * inner
    two_ref[...] = all_ref[:total, :].reshape(27, mid, out)
    pair = all_ref[total : total + first, :]
    one_ref[0:9] = pair[:, :mid].reshape(9, inner, mid)
    one_ref[9:18] = pair[:, mid:].reshape(9, inner, mid)
    pair = all_ref[total + first : total + first + first // 2, :]
    pair = jnp.concatenate([pair[:, :mid], pair[:, mid:]], axis=0)
    one_ref[18:27] = pair.reshape(9, inner, mid)
    tail = all_ref[plan.total - ROWS : plan.total - ROWS // 2, :] + all_ref[plan.total - ROWS // 2 : plan.total, :]
    bias_two_ref[...] = tail[0:1, :out]
    bias_one_ref[...] = tail[1:2, :mid]


class Plan:
    def __init__(self, volumes, kernel_first, kernel_second):
        self.space, self.sample = lax.axis_size("space"), lax.axis_size("sample")
        self.inner, self.mid, self.out = kernel_first.shape[2], kernel_first.shape[1], kernel_second.shape[1]
        self.owned = volumes.shape[0] // self.space
        self.part_blocks = volumes.shape[2] // LANES
        self.blocks = self.part_blocks * self.space
        self.halves = self.blocks // 8
        self.cores = 2
        self.groups = self.sample // self.cores
        cells = self.blocks * LANES * volumes.shape[0] * self.sample
        self.scale_one = 1.0 / math.sqrt(cells)
        self.scale_two = 1.0 / math.sqrt(cells // 8)
        used = 27 * self.mid + 9 * self.inner * 3 // 2 + ROWS
        step = ROWS * self.groups * self.cores
        self.total = -(-used // step) * step
        self.chunk = self.total // self.groups // self.cores


def call(kernel, plan, name, out_shapes, *args, scratch=(), limit=SMALL_LIMIT):
    return pl.pallas_call(
        functools.partial(kernel, plan),
        out_shape=[jax.ShapeDtypeStruct(s, d) for s, d in out_shapes],
        in_specs=[vmem()] * len(args),
        out_specs=[vmem()] * len(out_shapes),
        scratch_shapes=[pltpu.VMEM(s, d) for s, d in scratch],
        compiler_params=pltpu.CompilerParams(vmem_limit_bytes=limit),
        name=name,
    )(*args)


def swap(value, axis, k):
    return lax.ppermute(value, axis, [(i, i ^ k) for i in range(lax.axis_size(axis))])


def on_device(volumes, grad_out, kernel_first, bias_first, kernel_second, bias_second):
    plan = Plan(volumes, kernel_first, kernel_second)
    inner, mid, out = plan.inner, plan.mid, plan.out
    me = lax.axis_index("space")

    def piece(k):
        return lax.dynamic_slice_in_dim(volumes, (me ^ k) * plan.owned, plan.owned, axis=0)

    parts = [piece(0)] + [swap(piece(k), "space", k) for k in range(1, plan.space)]
    weights = prepare_weights(kernel_first, bias_first, kernel_second, bias_second)
    cells, small = plan.blocks * LANES, plan.halves * LANES
    share = plan.total // plan.cores
    scratch = (
        ((plan.blocks, inner, LANES), BF16),
        ((9 * inner + ROWS, cells), BF16),
        ((3 * mid, cells), F32),
        ((mid, cells), F32),
        ((plan.blocks * mid, 2 * LANES), BF16),
        ((3 * mid, cells), BF16),
        ((9 * mid + ROWS, small), BF16),
        ((3 * out, small), F32),
        ((3 * out, small), BF16),
        ((9 * out, small), BF16),
        ((3 * mid, small), F32),
        ((plan.total, LANES), F32),
    )
    features, keep, send = call(
        main_kernel,
        plan,
        "main",
        (((plan.owned, out, small), BF16), ((share, LANES), F32), ((share, LANES), BF16)),
        *parts,
        grad_out,
        *weights,
        scratch=scratch,
        limit=48 * 1024 * 1024,
    )
    chunk = (plan.chunk, LANES)
    got = swap(send, "sample", 1)
    own, *sends = call(core_sum_kernel, plan, "core_sum", ((chunk, F32),) + ((chunk, BF16),) * (plan.groups - 1), keep, got, scratch=(((share, LANES), F32),))
    gots = [swap(s, "sample", plan.cores * k) for k, s in enumerate(sends, start=1)]
    (partial,) = call(group_sum_kernel, plan, "group_sum", ((chunk, BF16),), own, *gots)
    gots = [swap(partial, "space", k) for k in range(1, plan.space)]
    (whole,) = call(space_sum_kernel, plan, "space_sum", ((chunk, BF16),), partial, *gots)
    gots = [swap(whole, "sample", plan.cores * k) for k in range(1, plan.groups)]
    (mine,) = call(gather_kernel, plan, "gather", (((share, LANES), BF16),), whole, *gots)
    other = swap(mine, "sample", 1)
    one, bias_one, two, bias_two = call(
        unpack_kernel,
        plan,
        "unpack",
        (((27, inner, mid), F32), ((1, mid), F32), ((27, mid, out), F32), ((1, out), F32)),
        mine,
        other,
        scratch=(((plan.total, LANES), F32),),
    )
    return (features, jnp.swapaxes(one, 1, 2), bias_one.reshape(mid), jnp.swapaxes(two, 1, 2), bias_two.reshape(out))


def solution(mesh):
    in_specs = (P("sample", None, "space"), P(("sample", "space"), None, None), P(), P(), P(), P())
    out_specs = (P(("sample", "space"), None, None), P(), P(), P(), P())
    return jax.shard_map(
        on_device, mesh=mesh, in_specs=in_specs, out_specs=out_specs, check_vma=False
    )
```

```python
import functools
import math

import jax
import jax.numpy as jnp
from jax import lax
from jax.experimental import pallas as pl
from jax.experimental.pallas import tpu as pltpu
from jax.sharding import PartitionSpec as P

SIDE = 8
LEAK_SLOPE = 0.3
LANES = 128
ROWS = 16
SMALL_LIMIT = 4 * 1024 * 1024
BF16 = jnp.bfloat16
F32 = jnp.float32


def vmem():
    return pl.BlockSpec(memory_space=pltpu.VMEM)


def lane_iota(rows):
    return lax.broadcasted_iota(jnp.int32, (rows, LANES), 1)


def turn(block, shift):
    return pltpu.roll(block, (-shift) % LANES, 1) if shift % LANES else block


def dot(left, right):
    return jnp.dot(left, right, preferred_element_type=F32)


def dot_lanes(left, right):
    return lax.dot_general(left, right, (((1,), (1,)), ((), ())), preferred_element_type=F32)


def in_plane(side, tap):
    high, wide = tap // 3 - 1, tap % 3 - 1
    lane = lane_iota(1)
    row, col = lane // side % side + high, lane % side + wide
    valid = (row >= 0) & (row < side) & (col >= 0) & (col < side)
    return valid, high * side + wide


def weights_kernel(first_ref, second_ref, bias_one_ref, bias_two_ref, conv_one_ref, conv_two_ref, back_ref, col_one_ref, col_two_ref):
    mid, out = first_ref.shape[2], second_ref.shape[2]
    inner, deep = first_ref.shape[1], second_ref.shape[1]

    def eye(size):
        row = lax.broadcasted_iota(jnp.int32, (size, size), 0)
        return row == lax.broadcasted_iota(jnp.int32, (size, size), 1)

    for a in range(3):
        taps = first_ref[9 * a : 9 * a + 9].reshape(9 * inner, mid)
        conv_one_ref[a * mid : (a + 1) * mid, :] = dot_lanes(eye(mid).astype(BF16), taps).astype(BF16)
        taps = second_ref[9 * a : 9 * a + 9].reshape(9 * deep, out)
        conv_two_ref[a * out : (a + 1) * out, :] = dot_lanes(eye(out).astype(BF16), taps).astype(BF16)
        for t in range(9):
            back_ref[a * deep : (a + 1) * deep, t * out : (t + 1) * out] = second_ref[9 * a + t]
    for row_ref, col_ref, size in ((bias_one_ref, col_one_ref, mid), (bias_two_ref, col_two_ref, out)):
        col = jnp.sum(jnp.where(eye(size), row_ref[...], 0.0), axis=1, keepdims=True)
        col_ref[...] = jnp.broadcast_to(col, (size, LANES))


def prepare_weights(kernel_first, bias_first, kernel_second, bias_second):
    first, second = jnp.swapaxes(kernel_first, 1, 2), jnp.swapaxes(kernel_second, 1, 2)
    inner, mid, out = first.shape[1], first.shape[2], second.shape[2]
    shapes = (
        ((3 * mid, 9 * inner), BF16),
        ((3 * out, 9 * mid), BF16),
        ((3 * mid, 9 * out), BF16),
        ((mid, LANES), F32),
        ((out, LANES), F32),
    )
    return pl.pallas_call(
        weights_kernel,
        out_shape=[jax.ShapeDtypeStruct(s, d) for s, d in shapes],
        in_specs=[vmem()] * 4,
        out_specs=[vmem()] * 5,
        compiler_params=pltpu.CompilerParams(vmem_limit_bytes=SMALL_LIMIT),
        name="weights",
    )(first, second, bias_first.reshape(1, -1), bias_second.reshape(1, -1))


def main_kernel(plan, *refs):
    parts, grad_ref, conv_one_ref, conv_two_ref, back_ref, col_one_ref, col_two_ref = (
        refs[: plan.space],
        *refs[plan.space : plan.space + 6],
    )
    feat_ref, keep_ref, send_ref = refs[plan.space + 6 : plan.space + 9]
    x_ref, s_one, t_one, slope_ref, lk_ref, d_one, s_two, t_two, d_two, sd_two, u_two, pay_ref = refs[plan.space + 9 :]
    inner, mid, out = plan.inner, plan.mid, plan.out
    blocks, halves = plan.blocks, plan.halves
    place, core = lax.axis_index("space"), lax.axis_index("sample") % plan.cores
    side, small = SIDE, SIDE // 2
    plane = side * side
    low = small * small
    lane = lane_iota(1)

    s_one[9 * inner :, :] = jnp.ones((ROWS, blocks * LANES), BF16)
    s_two[9 * mid :, :] = jnp.ones((ROWS, halves * LANES), BF16)
    cell = lax.broadcasted_iota(jnp.int32, (LANES, LANES), 0)
    lanes = lax.broadcasted_iota(jnp.int32, (LANES, LANES), 1)
    parent = (cell % plane // side // 2) * small + cell % side // 2
    pool = jnp.where(parent == lanes % low, 0.125, 0.0).astype(BF16)
    pool = jnp.concatenate([pool, pool], axis=0)
    parent = (lanes % plane // side // 2) * small + lanes % side // 2

    for volume in range(plan.owned):
        for k, part in zip(reversed(range(plan.space)), parts):
            start = (place ^ k) * plan.part_blocks
            for j in range(plan.part_blocks):
                x_ref[start + j] = part[volume, :, j * LANES : (j + 1) * LANES]

        for first_block in range(0, blocks, plan.part_blocks):
            for tap in range(9):
                valid, shift = in_plane(side, tap)
                for j in range(first_block, first_block + plan.part_blocks):
                    block = x_ref[j]
                    if shift:
                        block = jnp.where(valid, turn(block, shift), jnp.zeros_like(block))
                    s_one[tap * inner : (tap + 1) * inner, j * LANES : (j + 1) * LANES] = block
            here = slice(first_block * LANES, (first_block + plan.part_blocks) * LANES)
            t_one[:, here] = dot(conv_one_ref[...], s_one[: 9 * inner, here])

        upper = lane >= plane
        for j in range(blocks):
            here = slice(j * LANES, (j + 1) * LANES)
            before, after = slice(here.start - LANES, here.start), slice(here.stop, here.stop + LANES)
            zero = jnp.zeros((mid, LANES), F32)
            up = jnp.where(upper, t_one[:mid, before] if j else zero, t_one[:mid, here])
            down = jnp.where(upper, t_one[2 * mid :, here], t_one[2 * mid :, after] if j < blocks - 1 else zero)
            pre = t_one[mid : 2 * mid, here] + turn(up + down, plane) + col_one_ref[...]
            slope = jnp.where(pre > 0, 1.0, LEAK_SLOPE)
            slope_ref[:, here] = slope * 0.125
            value = slope * pre
            high = value.astype(BF16)
            lk_ref[j * mid : (j + 1) * mid, :LANES] = high
            lk_ref[j * mid : (j + 1) * mid, LANES:] = (value - high.astype(F32)).astype(BF16)

        means = dot(lk_ref[...], pool)
        for h in range(halves):
            here = slice(h * LANES, (h + 1) * LANES)
            pooled = jnp.zeros((mid, LANES), F32)
            for j in range(LANES // low):
                row = (h * (LANES // low) + j) * mid
                pooled = jnp.where(lane // low == j, means[row : row + mid], pooled)
            for tap in range(9):
                valid, shift = in_plane(small, tap)
                block = jnp.where(valid, turn(pooled, shift), 0.0) if shift else pooled
                s_two[tap * mid : (tap + 1) * mid, here] = block.astype(BF16)

        t_two[...] = dot(conv_two_ref[...], s_two[: 9 * mid, :])
        deltas = []
        for h in range(halves):
            here = slice(h * LANES, (h + 1) * LANES)
            before, after = slice(here.start - LANES, here.start), slice(here.stop, here.stop + LANES)
            zero = jnp.zeros((out, LANES), F32)
            up = jnp.where(lane >= LANES - low, t_two[:out, before] if h else zero, t_two[:out, here])
            down = jnp.where(lane < low, t_two[2 * out :, after] if h < halves - 1 else zero, t_two[2 * out :, here])
            pre = t_two[out : 2 * out, here] + turn(up, -low) + turn(down, low) + col_two_ref[...]
            slope = jnp.where(pre > 0, 1.0, LEAK_SLOPE)
            feat_ref[volume, :, here] = (slope * pre).astype(BF16)
            delta = (grad_ref[volume, :, here].astype(F32) * slope).astype(BF16).astype(F32)
            deltas.append(delta)
            for tap in range(9):
                valid, shift = in_plane(small, 8 - tap)
                block = jnp.where(valid, turn(delta, shift), 0.0) if shift else delta
                sd_two[tap * out : (tap + 1) * out, here] = block.astype(BF16)

        for h in range(halves):
            here = slice(h * LANES, (h + 1) * LANES)
            zero = jnp.zeros((out, LANES), F32)
            after = deltas[h + 1] if h < halves - 1 else zero
            before = deltas[h - 1] if h else zero
            d_two[:out, here] = turn(jnp.where(lane < low, after, deltas[h]), low).astype(BF16)
            d_two[out : 2 * out, here] = deltas[h].astype(BF16)
            d_two[2 * out :, here] = turn(jnp.where(lane >= LANES - low, before, deltas[h]), -low).astype(BF16)

        u_two[...] = dot(back_ref[...], sd_two[...])
        spreads = []
        for h in range(halves):
            here = slice(h * LANES, (h + 1) * LANES)
            before, after = slice(here.start - LANES, here.start), slice(here.stop, here.stop + LANES)
            zero = jnp.zeros((mid, LANES), F32)
            down = jnp.where(lane < low, u_two[:mid, after] if h < halves - 1 else zero, u_two[:mid, here])
            up = jnp.where(lane >= LANES - low, u_two[2 * mid :, before] if h else zero, u_two[2 * mid :, here])
            spreads.append((u_two[mid : 2 * mid, here] + turn(down, low) + turn(up, -low)).astype(BF16))
        spread = jnp.concatenate(spreads, axis=0)

        deltas = []
        for j in range(LANES // low):
            unpool = jnp.where(parent + j * low == cell, 1.0, 0.0).astype(BF16)
            deltas.append(dot(spread, unpool))
        wide = []
        for j in range(blocks):
            here = slice(j * LANES, (j + 1) * LANES)
            h, i = j // (LANES // low), j % (LANES // low)
            wide.append(deltas[i][h * mid : (h + 1) * mid] * slope_ref[:, here])
        for j in range(blocks):
            here = slice(j * LANES, (j + 1) * LANES)
            zero = jnp.zeros((mid, LANES), F32)
            after = wide[j + 1] if j < blocks - 1 else zero
            before = wide[j - 1] if j else zero
            d_one[:mid, here] = turn(jnp.where(upper, wide[j], after), plane).astype(BF16)
            d_one[mid : 2 * mid, here] = wide[j].astype(BF16)
            d_one[2 * mid :, here] = turn(jnp.where(upper, before, wide[j]), plane).astype(BF16)

        two = dot_lanes(s_two[...], d_two[...]) * plan.scale_two
        one = dot_lanes(s_one[...], d_one[...]) * plan.scale_one
        first = 9 * inner
        total = 27 * mid
        half = first // 2
        pieces = [(a * 9 * mid, two[: 9 * mid, a * out : (a + 1) * out]) for a in range(3)]
        pieces.append((total, one[:first, : 2 * mid]))
        pieces.append((total + first, jnp.concatenate([one[:half, 2 * mid :], one[half:first, 2 * mid :]], axis=1)))
        row = lax.broadcasted_iota(jnp.int32, (ROWS // 2, LANES), 0)
        own = one[first : first + ROWS // 2, : 2 * mid]
        own = jnp.where(lane_iota(1) < mid, turn(own, mid), 0.0)
        tail = jnp.where(row == 0, two[9 * mid : 9 * mid + ROWS // 2, out : 2 * out], jnp.where(row == 1, own, 0.0))
        if volume:
            tail = tail + pay_ref[plan.total - ROWS : plan.total - ROWS // 2] + pay_ref[plan.total - ROWS // 2 :]
        for start, piece in pieces:
            span = slice(start, start + piece.shape[0])
            pay_ref[span, :] = piece + pay_ref[span, :] if volume else piece
        used = total + first + half
        if not volume and used < plan.total - ROWS:
            pay_ref[used : plan.total - ROWS, :] = jnp.zeros((plan.total - ROWS - used, LANES), F32)
        high = tail.astype(BF16).astype(F32)
        pay_ref[plan.total - ROWS :, :] = jnp.concatenate([high, tail - high], axis=0)

    share = plan.total // plan.cores
    keep_ref[...] = pay_ref[pl.ds(pl.multiple_of(core * share, ROWS), share), :]
    send_ref[...] = pay_ref[pl.ds(pl.multiple_of((1 - core) * share, ROWS), share), :].astype(BF16)


def split_again(values, plan, last):
    rows = values.shape[0]
    tail = values[rows - ROWS : rows - ROWS // 2] + values[rows - ROWS // 2 :]
    high = tail.astype(BF16).astype(F32)
    parted = jnp.concatenate([high, tail - high], axis=0)
    return jnp.where(last, parted, values[rows - ROWS :])


def core_sum_kernel(plan, keep_ref, got_ref, own_ref, *rest):
    sends, sum_ref = rest[:-1], rest[-1]
    group = lax.axis_index("sample") // plan.cores
    core = lax.axis_index("sample") % plan.cores
    rows = keep_ref.shape[0]
    sum_ref[...] = keep_ref[...] + got_ref[...].astype(F32)
    sum_ref[rows - ROWS :, :] = split_again(sum_ref[rows - ROWS :, :], plan, core == plan.cores - 1)

    def chunk(k):
        return sum_ref[pl.ds(pl.multiple_of((group ^ k) * plan.chunk, ROWS), plan.chunk), :]

    own_ref[...] = chunk(0)
    for k, send in enumerate(sends, start=1):
        send[...] = chunk(k).astype(BF16)


def last_chunk(plan):
    return lax.axis_index("sample") == lax.axis_size("sample") - 1


def group_sum_kernel(plan, own_ref, *rest):
    gots, out_ref = rest[:-1], rest[-1]
    total = own_ref[...]
    for got in gots:
        total = total + got[...].astype(F32)
    rows = total.shape[0]
    out_ref[: rows - ROWS, :] = total[: rows - ROWS].astype(BF16)
    out_ref[rows - ROWS :, :] = split_again(total[rows - ROWS :], plan, last_chunk(plan)).astype(BF16)


def space_sum_kernel(plan, *refs):
    values, out_ref = [ref[...].astype(F32) for ref in refs[:-1]], refs[-1]
    while len(values) > 1:
        values = [values[i] + values[i + 1] for i in range(0, len(values), 2)]
    total = values[0]
    rows = total.shape[0]
    out_ref[: rows - ROWS, :] = total[: rows - ROWS].astype(BF16)
    out_ref[rows - ROWS :, :] = split_again(total[rows - ROWS :], plan, last_chunk(plan)).astype(BF16)


def unpack_kernel(plan, *refs):
    one_ref, bias_one_ref, two_ref, bias_two_ref, all_ref = refs[-5:]
    inner, mid, out = plan.inner, plan.mid, plan.out
    group, core = lax.axis_index("sample") // plan.cores, lax.axis_index("sample") % plan.cores
    for k, ref in enumerate(refs[:-5]):
        side, k = k // plan.groups, k % plan.groups
        start = ((core ^ side) * plan.groups + (group ^ k)) * plan.chunk
        all_ref[pl.ds(pl.multiple_of(start, ROWS), plan.chunk), :] = ref[...].astype(F32)
    total, first = 27 * mid, 9 * inner
    two_ref[...] = all_ref[:total, :].reshape(27, mid, out)
    pair = all_ref[total : total + first, :]
    one_ref[0:9] = pair[:, :mid].reshape(9, inner, mid)
    one_ref[9:18] = pair[:, mid:].reshape(9, inner, mid)
    pair = all_ref[total + first : total + first + first // 2, :]
    pair = jnp.concatenate([pair[:, :mid], pair[:, mid:]], axis=0)
    one_ref[18:27] = pair.reshape(9, inner, mid)
    tail = all_ref[plan.total - ROWS : plan.total - ROWS // 2, :] + all_ref[plan.total - ROWS // 2 : plan.total, :]
    bias_two_ref[...] = tail[0:1, :out]
    bias_one_ref[...] = tail[1:2, :mid]


class Plan:
    def __init__(self, volumes, kernel_first, kernel_second):
        self.space, self.sample = lax.axis_size("space"), lax.axis_size("sample")
        self.inner, self.mid, self.out = kernel_first.shape[2], kernel_first.shape[1], kernel_second.shape[1]
        self.owned = volumes.shape[0] // self.space
        self.part_blocks = volumes.shape[2] // LANES
        self.blocks = self.part_blocks * self.space
        self.halves = self.blocks // 8
        self.cores = 2
        self.groups = self.sample // self.cores
        cells = self.blocks * LANES * volumes.shape[0] * self.sample
        self.scale_one = 1.0 / math.sqrt(cells)
        self.scale_two = 1.0 / math.sqrt(cells // 8)
        used = 27 * self.mid + 9 * self.inner * 3 // 2 + ROWS
        step = ROWS * self.groups * self.cores
        self.total = -(-used // step) * step
        self.chunk = self.total // self.groups // self.cores


def call(kernel, plan, name, out_shapes, *args, scratch=(), limit=SMALL_LIMIT):
    return pl.pallas_call(
        functools.partial(kernel, plan),
        out_shape=[jax.ShapeDtypeStruct(s, d) for s, d in out_shapes],
        in_specs=[vmem()] * len(args),
        out_specs=[vmem()] * len(out_shapes),
        scratch_shapes=[pltpu.VMEM(s, d) for s, d in scratch],
        compiler_params=pltpu.CompilerParams(vmem_limit_bytes=limit),
        name=name,
    )(*args)


def swap(value, axis, k):
    return lax.ppermute(value, axis, [(i, i ^ k) for i in range(lax.axis_size(axis))])


def on_device(volumes, grad_out, kernel_first, bias_first, kernel_second, bias_second):
    plan = Plan(volumes, kernel_first, kernel_second)
    inner, mid, out = plan.inner, plan.mid, plan.out
    me = lax.axis_index("space")

    def piece(k):
        return lax.dynamic_slice_in_dim(volumes, (me ^ k) * plan.owned, plan.owned, axis=0)

    parts = [piece(0)] + [swap(piece(k), "space", k) for k in range(1, plan.space)]
    weights = prepare_weights(kernel_first, bias_first, kernel_second, bias_second)
    cells, small = plan.blocks * LANES, plan.halves * LANES
    share = plan.total // plan.cores
    scratch = (
        ((plan.blocks, inner, LANES), BF16),
        ((9 * inner + ROWS, cells), BF16),
        ((3 * mid, cells), F32),
        ((mid, cells), F32),
        ((plan.blocks * mid, 2 * LANES), BF16),
        ((3 * mid, cells), BF16),
        ((9 * mid + ROWS, small), BF16),
        ((3 * out, small), F32),
        ((3 * out, small), BF16),
        ((9 * out, small), BF16),
        ((3 * mid, small), F32),
        ((plan.total, LANES), F32),
    )
    features, keep, send = call(
        main_kernel,
        plan,
        "main",
        (((plan.owned, out, small), BF16), ((share, LANES), F32), ((share, LANES), BF16)),
        *reversed(parts),
        grad_out,
        *weights,
        scratch=scratch,
        limit=48 * 1024 * 1024,
    )
    chunk = (plan.chunk, LANES)
    got = swap(send, "sample", 1)
    own, *sends = call(core_sum_kernel, plan, "core_sum", ((chunk, F32),) + ((chunk, BF16),) * (plan.groups - 1), keep, got, scratch=(((share, LANES), F32),))
    gots = [swap(s, "sample", plan.cores * k) for k, s in enumerate(sends, start=1)]
    (partial,) = call(group_sum_kernel, plan, "group_sum", ((chunk, BF16),), own, *gots[1:], gots[0])
    gots = [swap(partial, "space", k ^ (k >> 1)) for k in range(1, plan.space)]
    (whole,) = call(space_sum_kernel, plan, "space_sum", ((chunk, BF16),), partial, *gots)
    gots = [swap(whole, "sample", plan.cores * k) for k in range(1, plan.groups)]
    mine = [whole, *gots]
    other = [swap(value, "sample", 1) for value in mine]
    one, bias_one, two, bias_two = call(
        unpack_kernel,
        plan,
        "unpack",
        (((27, inner, mid), F32), ((1, mid), F32), ((27, mid, out), F32), ((1, out), F32)),
        *mine,
        *other,
        scratch=(((plan.total, LANES), F32),),
    )
    return (features, jnp.swapaxes(one, 1, 2), bias_one.reshape(mid), jnp.swapaxes(two, 1, 2), bias_two.reshape(out))


def solution(mesh):
    in_specs = (P("sample", None, "space"), P(("sample", "space"), None, None), P(), P(), P(), P())
    out_specs = (P(("sample", "space"), None, None), P(), P(), P(), P())
    return jax.shard_map(
        on_device, mesh=mesh, in_specs=in_specs, out_specs=out_specs, check_vma=False
    )
```

```python
import functools
import math

import jax
import jax.numpy as jnp
from jax import lax
from jax.experimental import pallas as pl
from jax.experimental.pallas import tpu as pltpu
from jax.sharding import PartitionSpec as P

SIDE = 8
LEAK_SLOPE = 0.3
LANES = 128
ROWS = 16
SMALL_LIMIT = 4 * 1024 * 1024
BF16 = jnp.bfloat16
F32 = jnp.float32


def gray(number):
    return number ^ (number >> 1)


def odd(number):
    for shift in (8, 4, 2, 1):
        number = number ^ (number >> shift)
    return number & 1


def half_of(plan, sample):
    return (sample % plan.cores) ^ odd(sample // plan.cores)


def own_half(plan):
    return half_of(plan, lax.axis_index("sample"))


def place_in(plan, half):
    group, space = lax.axis_index("sample") // plan.cores, lax.axis_index("space")
    return jnp.where(half == 0, group, space) if plan.crossed else group


def vmem():
    return pl.BlockSpec(memory_space=pltpu.VMEM)


def lane_iota(rows):
    return lax.broadcasted_iota(jnp.int32, (rows, LANES), 1)


def turn(block, shift):
    return pltpu.roll(block, (-shift) % LANES, 1) if shift % LANES else block


def dot(left, right):
    return jnp.dot(left, right, preferred_element_type=F32)


def dot_lanes(left, right):
    return lax.dot_general(left, right, (((1,), (1,)), ((), ())), preferred_element_type=F32)


def in_plane(side, tap):
    high, wide = tap // 3 - 1, tap % 3 - 1
    lane = lane_iota(1)
    row, col = lane // side % side + high, lane % side + wide
    valid = (row >= 0) & (row < side) & (col >= 0) & (col < side)
    return valid, high * side + wide


def weights_kernel(first_ref, second_ref, bias_one_ref, bias_two_ref, conv_one_ref, conv_two_ref, back_ref, col_one_ref, col_two_ref):
    mid, out = first_ref.shape[2], second_ref.shape[2]
    inner, deep = first_ref.shape[1], second_ref.shape[1]

    def eye(size):
        row = lax.broadcasted_iota(jnp.int32, (size, size), 0)
        return row == lax.broadcasted_iota(jnp.int32, (size, size), 1)

    for a in range(3):
        taps = first_ref[9 * a : 9 * a + 9].reshape(9 * inner, mid)
        conv_one_ref[a * mid : (a + 1) * mid, :] = dot_lanes(eye(mid).astype(BF16), taps).astype(BF16)
        taps = second_ref[9 * a : 9 * a + 9].reshape(9 * deep, out)
        conv_two_ref[a * out : (a + 1) * out, :] = dot_lanes(eye(out).astype(BF16), taps).astype(BF16)
        for t in range(9):
            back_ref[a * deep : (a + 1) * deep, t * out : (t + 1) * out] = second_ref[9 * a + t]
    for row_ref, col_ref, size in ((bias_one_ref, col_one_ref, mid), (bias_two_ref, col_two_ref, out)):
        col = jnp.sum(jnp.where(eye(size), row_ref[...], 0.0), axis=1, keepdims=True)
        col_ref[...] = jnp.broadcast_to(col, (size, LANES))


def prepare_weights(kernel_first, bias_first, kernel_second, bias_second):
    first, second = jnp.swapaxes(kernel_first, 1, 2), jnp.swapaxes(kernel_second, 1, 2)
    inner, mid, out = first.shape[1], first.shape[2], second.shape[2]
    shapes = (
        ((3 * mid, 9 * inner), BF16),
        ((3 * out, 9 * mid), BF16),
        ((3 * mid, 9 * out), BF16),
        ((mid, LANES), F32),
        ((out, LANES), F32),
    )
    return pl.pallas_call(
        weights_kernel,
        out_shape=[jax.ShapeDtypeStruct(s, d) for s, d in shapes],
        in_specs=[vmem()] * 4,
        out_specs=[vmem()] * 5,
        compiler_params=pltpu.CompilerParams(vmem_limit_bytes=SMALL_LIMIT),
        name="weights",
    )(first, second, bias_first.reshape(1, -1), bias_second.reshape(1, -1))


def main_kernel(plan, *refs):
    parts, grad_ref, conv_one_ref, conv_two_ref, back_ref, col_one_ref, col_two_ref = (
        refs[: plan.space],
        *refs[plan.space : plan.space + 6],
    )
    feat_ref, keep_ref, send_ref = refs[plan.space + 6 : plan.space + 9]
    x_ref, s_one, t_one, slope_ref, lk_ref, d_one, s_two, t_two, d_two, sd_two, u_two, pay_ref = refs[plan.space + 9 :]
    inner, mid, out = plan.inner, plan.mid, plan.out
    blocks, halves = plan.blocks, plan.halves
    place, own_core = lax.axis_index("space"), own_half(plan)
    side, small = SIDE, SIDE // 2
    plane = side * side
    low = small * small
    lane = lane_iota(1)

    s_one[9 * inner :, :] = jnp.ones((ROWS, blocks * LANES), BF16)
    s_two[9 * mid :, :] = jnp.ones((ROWS, halves * LANES), BF16)
    cell = lax.broadcasted_iota(jnp.int32, (LANES, LANES), 0)
    lanes = lax.broadcasted_iota(jnp.int32, (LANES, LANES), 1)
    parent = (cell % plane // side // 2) * small + cell % side // 2
    pool = jnp.where(parent == lanes % low, 0.125, 0.0).astype(BF16)
    pool = jnp.concatenate([pool, pool], axis=0)
    parent = (lanes % plane // side // 2) * small + lanes % side // 2

    for volume in range(plan.owned):
        for k, part in zip(reversed(range(plan.space)), parts):
            start = (place ^ k) * plan.part_blocks
            for j in range(plan.part_blocks):
                x_ref[start + j] = part[volume, :, j * LANES : (j + 1) * LANES]

        for first_block in range(0, blocks, plan.part_blocks):
            for tap in range(9):
                valid, shift = in_plane(side, tap)
                for j in range(first_block, first_block + plan.part_blocks):
                    block = x_ref[j]
                    if shift:
                        block = jnp.where(valid, turn(block, shift), jnp.zeros_like(block))
                    s_one[tap * inner : (tap + 1) * inner, j * LANES : (j + 1) * LANES] = block
            here = slice(first_block * LANES, (first_block + plan.part_blocks) * LANES)
            t_one[:, here] = dot(conv_one_ref[...], s_one[: 9 * inner, here])

        upper = lane >= plane
        for j in range(blocks):
            here = slice(j * LANES, (j + 1) * LANES)
            before, after = slice(here.start - LANES, here.start), slice(here.stop, here.stop + LANES)
            zero = jnp.zeros((mid, LANES), F32)
            up = jnp.where(upper, t_one[:mid, before] if j else zero, t_one[:mid, here])
            down = jnp.where(upper, t_one[2 * mid :, here], t_one[2 * mid :, after] if j < blocks - 1 else zero)
            pre = t_one[mid : 2 * mid, here] + turn(up + down, plane) + col_one_ref[...]
            slope = jnp.where(pre > 0, 1.0, LEAK_SLOPE)
            slope_ref[:, here] = slope * 0.125
            value = slope * pre
            high = value.astype(BF16)
            lk_ref[j * mid : (j + 1) * mid, :LANES] = high
            lk_ref[j * mid : (j + 1) * mid, LANES:] = (value - high.astype(F32)).astype(BF16)

        means = dot(lk_ref[...], pool)
        for h in range(halves):
            here = slice(h * LANES, (h + 1) * LANES)
            pooled = jnp.zeros((mid, LANES), F32)
            for j in range(LANES // low):
                row = (h * (LANES // low) + j) * mid
                pooled = jnp.where(lane // low == j, means[row : row + mid], pooled)
            for tap in range(9):
                valid, shift = in_plane(small, tap)
                block = jnp.where(valid, turn(pooled, shift), 0.0) if shift else pooled
                s_two[tap * mid : (tap + 1) * mid, here] = block.astype(BF16)

        t_two[...] = dot(conv_two_ref[...], s_two[: 9 * mid, :])
        deltas = []
        for h in range(halves):
            here = slice(h * LANES, (h + 1) * LANES)
            before, after = slice(here.start - LANES, here.start), slice(here.stop, here.stop + LANES)
            zero = jnp.zeros((out, LANES), F32)
            up = jnp.where(lane >= LANES - low, t_two[:out, before] if h else zero, t_two[:out, here])
            down = jnp.where(lane < low, t_two[2 * out :, after] if h < halves - 1 else zero, t_two[2 * out :, here])
            pre = t_two[out : 2 * out, here] + turn(up, -low) + turn(down, low) + col_two_ref[...]
            slope = jnp.where(pre > 0, 1.0, LEAK_SLOPE)
            feat_ref[volume, :, here] = (slope * pre).astype(BF16)
            delta = (grad_ref[volume, :, here].astype(F32) * slope).astype(BF16).astype(F32)
            deltas.append(delta)
            for tap in range(9):
                valid, shift = in_plane(small, 8 - tap)
                block = jnp.where(valid, turn(delta, shift), 0.0) if shift else delta
                sd_two[tap * out : (tap + 1) * out, here] = block.astype(BF16)

        for h in range(halves):
            here = slice(h * LANES, (h + 1) * LANES)
            zero = jnp.zeros((out, LANES), F32)
            after = deltas[h + 1] if h < halves - 1 else zero
            before = deltas[h - 1] if h else zero
            d_two[:out, here] = turn(jnp.where(lane < low, after, deltas[h]), low).astype(BF16)
            d_two[out : 2 * out, here] = deltas[h].astype(BF16)
            d_two[2 * out :, here] = turn(jnp.where(lane >= LANES - low, before, deltas[h]), -low).astype(BF16)

        u_two[...] = dot(back_ref[...], sd_two[...])
        spreads = []
        for h in range(halves):
            here = slice(h * LANES, (h + 1) * LANES)
            before, after = slice(here.start - LANES, here.start), slice(here.stop, here.stop + LANES)
            zero = jnp.zeros((mid, LANES), F32)
            down = jnp.where(lane < low, u_two[:mid, after] if h < halves - 1 else zero, u_two[:mid, here])
            up = jnp.where(lane >= LANES - low, u_two[2 * mid :, before] if h else zero, u_two[2 * mid :, here])
            spreads.append((u_two[mid : 2 * mid, here] + turn(down, low) + turn(up, -low)).astype(BF16))
        spread = jnp.concatenate(spreads, axis=0)

        deltas = []
        for j in range(LANES // low):
            unpool = jnp.where(parent + j * low == cell, 1.0, 0.0).astype(BF16)
            deltas.append(dot(spread, unpool))
        wide = []
        for j in range(blocks):
            here = slice(j * LANES, (j + 1) * LANES)
            h, i = j // (LANES // low), j % (LANES // low)
            wide.append(deltas[i][h * mid : (h + 1) * mid] * slope_ref[:, here])
        for j in range(blocks):
            here = slice(j * LANES, (j + 1) * LANES)
            zero = jnp.zeros((mid, LANES), F32)
            after = wide[j + 1] if j < blocks - 1 else zero
            before = wide[j - 1] if j else zero
            d_one[:mid, here] = turn(jnp.where(upper, wide[j], after), plane).astype(BF16)
            d_one[mid : 2 * mid, here] = wide[j].astype(BF16)
            d_one[2 * mid :, here] = turn(jnp.where(upper, before, wide[j]), plane).astype(BF16)

        two = dot_lanes(s_two[...], d_two[...]) * plan.scale_two
        one = dot_lanes(s_one[...], d_one[...]) * plan.scale_one
        first = 9 * inner
        total = 27 * mid
        half = first // 2
        pieces = [(a * 9 * mid, two[: 9 * mid, a * out : (a + 1) * out]) for a in range(3)]
        pieces.append((total, one[:first, : 2 * mid]))
        pieces.append((total + first, jnp.concatenate([one[:half, 2 * mid :], one[half:first, 2 * mid :]], axis=1)))
        row = lax.broadcasted_iota(jnp.int32, (ROWS // 2, LANES), 0)
        own = one[first : first + ROWS // 2, : 2 * mid]
        own = jnp.where(lane_iota(1) < mid, turn(own, mid), 0.0)
        tail = jnp.where(row == 0, two[9 * mid : 9 * mid + ROWS // 2, out : 2 * out], jnp.where(row == 1, own, 0.0))
        if volume:
            tail = tail + pay_ref[plan.total - ROWS : plan.total - ROWS // 2] + pay_ref[plan.total - ROWS // 2 :]
        for start, piece in pieces:
            span = slice(start, start + piece.shape[0])
            pay_ref[span, :] = piece + pay_ref[span, :] if volume else piece
        used = total + first + half
        if not volume and used < plan.total - ROWS:
            pay_ref[used : plan.total - ROWS, :] = jnp.zeros((plan.total - ROWS - used, LANES), F32)
        high = tail.astype(BF16).astype(F32)
        pay_ref[plan.total - ROWS :, :] = jnp.concatenate([high, tail - high], axis=0)

    share = plan.total // plan.cores
    keep_ref[...] = pay_ref[pl.ds(pl.multiple_of(own_core * share, ROWS), share), :]
    send_ref[...] = pay_ref[pl.ds(pl.multiple_of((1 - own_core) * share, ROWS), share), :].astype(BF16)


def split_again(values, plan, last):
    rows = values.shape[0]
    tail = values[rows - ROWS : rows - ROWS // 2] + values[rows - ROWS // 2 :]
    high = tail.astype(BF16).astype(F32)
    parted = jnp.concatenate([high, tail - high], axis=0)
    return jnp.where(last, parted, values[rows - ROWS :])


def core_sum_kernel(plan, keep_ref, got_ref, own_ref, *rest):
    sends, sum_ref = rest[:-1], rest[-1]
    half = own_half(plan)
    place = place_in(plan, half)
    rows = keep_ref.shape[0]
    sum_ref[...] = keep_ref[...] + got_ref[...].astype(F32)
    sum_ref[rows - ROWS :, :] = split_again(sum_ref[rows - ROWS :, :], plan, half == plan.cores - 1)

    def chunk(k):
        return sum_ref[pl.ds(pl.multiple_of((place ^ k) * plan.chunk, ROWS), plan.chunk), :]

    own_ref[...] = chunk(0)
    for k, send in enumerate(sends, start=1):
        send[...] = chunk(k).astype(BF16)


def last_chunk(plan):
    half = own_half(plan)
    return (half == plan.cores - 1) & (place_in(plan, half) == plan.groups - 1)


def group_sum_kernel(plan, own_ref, *rest):
    gots, out_ref = rest[:-1], rest[-1]
    total = own_ref[...]
    for got in gots:
        total = total + got[...].astype(F32)
    rows = total.shape[0]
    out_ref[: rows - ROWS, :] = total[: rows - ROWS].astype(BF16)
    out_ref[rows - ROWS :, :] = split_again(total[rows - ROWS :], plan, last_chunk(plan)).astype(BF16)


def space_sum_kernel(plan, *refs):
    values, out_ref = [ref[...].astype(F32) for ref in refs[:-1]], refs[-1]
    while len(values) > 1:
        values = [values[i] + values[i + 1] for i in range(0, len(values), 2)]
    total = values[0]
    rows = total.shape[0]
    out_ref[: rows - ROWS, :] = total[: rows - ROWS].astype(BF16)
    out_ref[rows - ROWS :, :] = split_again(total[rows - ROWS :], plan, last_chunk(plan)).astype(BF16)


def unpack_kernel(plan, *refs):
    one_ref, bias_one_ref, two_ref, bias_two_ref, all_ref = refs[-5:]
    inner, mid, out = plan.inner, plan.mid, plan.out
    own = own_half(plan)
    for k, ref in enumerate(refs[:-5]):
        side, k = k // plan.groups, k % plan.groups
        start = ((own ^ side) * plan.groups + (place_in(plan, own ^ side) ^ gray(k))) * plan.chunk
        all_ref[pl.ds(pl.multiple_of(start, ROWS), plan.chunk), :] = ref[...].astype(F32)
    total, first = 27 * mid, 9 * inner
    two_ref[...] = all_ref[:total, :].reshape(27, mid, out)
    pair = all_ref[total : total + first, :]
    one_ref[0:9] = pair[:, :mid].reshape(9, inner, mid)
    one_ref[9:18] = pair[:, mid:].reshape(9, inner, mid)
    pair = all_ref[total + first : total + first + first // 2, :]
    pair = jnp.concatenate([pair[:, :mid], pair[:, mid:]], axis=0)
    one_ref[18:27] = pair.reshape(9, inner, mid)
    tail = all_ref[plan.total - ROWS : plan.total - ROWS // 2, :] + all_ref[plan.total - ROWS // 2 : plan.total, :]
    bias_two_ref[...] = tail[0:1, :out]
    bias_one_ref[...] = tail[1:2, :mid]


class Plan:
    def __init__(self, volumes, kernel_first, kernel_second):
        self.space, self.sample = lax.axis_size("space"), lax.axis_size("sample")
        self.inner, self.mid, self.out = kernel_first.shape[2], kernel_first.shape[1], kernel_second.shape[1]
        self.owned = volumes.shape[0] // self.space
        self.part_blocks = volumes.shape[2] // LANES
        self.blocks = self.part_blocks * self.space
        self.halves = self.blocks // 8
        self.cores = 2
        self.groups = self.sample // self.cores
        self.crossed = self.groups == self.space
        cells = self.blocks * LANES * volumes.shape[0] * self.sample
        self.scale_one = 1.0 / math.sqrt(cells)
        self.scale_two = 1.0 / math.sqrt(cells // 8)
        used = 27 * self.mid + 9 * self.inner * 3 // 2 + ROWS
        step = ROWS * self.groups * self.cores
        self.total = -(-used // step) * step
        self.chunk = self.total // self.groups // self.cores


def call(kernel, plan, name, out_shapes, *args, scratch=(), limit=SMALL_LIMIT):
    return pl.pallas_call(
        functools.partial(kernel, plan),
        out_shape=[jax.ShapeDtypeStruct(s, d) for s, d in out_shapes],
        in_specs=[vmem()] * len(args),
        out_specs=[vmem()] * len(out_shapes),
        scratch_shapes=[pltpu.VMEM(s, d) for s, d in scratch],
        compiler_params=pltpu.CompilerParams(vmem_limit_bytes=limit),
        name=name,
    )(*args)


def swap(value, axis, k):
    return lax.ppermute(value, axis, [(i, i ^ k) for i in range(lax.axis_size(axis))])


def trade(plan, value, k, within):
    pairs = []
    for sample in range(plan.sample):
        for space in range(plan.space):
            half = half_of(plan, sample)
            group, other = sample // plan.cores, space
            if (plan.crossed and half == 1) == within:
                other = other ^ k
            else:
                group = group ^ k
            core = half ^ half_of(plan, group * plan.cores)
            pairs.append((sample * plan.space + space, (group * plan.cores + core) * plan.space + other))
    return lax.ppermute(value, ("sample", "space"), pairs)


def on_device(volumes, grad_out, kernel_first, bias_first, kernel_second, bias_second):
    plan = Plan(volumes, kernel_first, kernel_second)
    inner, mid, out = plan.inner, plan.mid, plan.out
    me = lax.axis_index("space")

    def piece(k):
        return lax.dynamic_slice_in_dim(volumes, (me ^ k) * plan.owned, plan.owned, axis=0)

    parts = [piece(0)] + [swap(piece(k), "space", k) for k in range(1, plan.space)]
    weights = prepare_weights(kernel_first, bias_first, kernel_second, bias_second)
    cells, small = plan.blocks * LANES, plan.halves * LANES
    share = plan.total // plan.cores
    scratch = (
        ((plan.blocks, inner, LANES), BF16),
        ((9 * inner + ROWS, cells), BF16),
        ((3 * mid, cells), F32),
        ((mid, cells), F32),
        ((plan.blocks * mid, 2 * LANES), BF16),
        ((3 * mid, cells), BF16),
        ((9 * mid + ROWS, small), BF16),
        ((3 * out, small), F32),
        ((3 * out, small), BF16),
        ((9 * out, small), BF16),
        ((3 * mid, small), F32),
        ((plan.total, LANES), F32),
    )
    features, keep, send = call(
        main_kernel,
        plan,
        "main",
        (((plan.owned, out, small), BF16), ((share, LANES), F32), ((share, LANES), BF16)),
        *reversed(parts),
        grad_out,
        *weights,
        scratch=scratch,
        limit=48 * 1024 * 1024,
    )
    chunk = (plan.chunk, LANES)
    got = swap(send, "sample", 1)
    own, *sends = call(core_sum_kernel, plan, "core_sum", ((chunk, F32),) + ((chunk, BF16),) * (plan.groups - 1), keep, got, scratch=(((share, LANES), F32),))
    gots = [trade(plan, s, k, True) for k, s in enumerate(sends, start=1)]
    (partial,) = call(group_sum_kernel, plan, "group_sum", ((chunk, BF16),), own, *gots[1:], gots[0])
    gots = [trade(plan, partial, gray(k), False) for k in range(1, plan.space)]
    (whole,) = call(space_sum_kernel, plan, "space_sum", ((chunk, BF16),), partial, *gots)
    mine = [whole] + [trade(plan, whole, gray(k), True) for k in range(1, plan.groups)]
    other = [swap(value, "sample", 1) for value in mine]
    one, bias_one, two, bias_two = call(
        unpack_kernel,
        plan,
        "unpack",
        (((27, inner, mid), F32), ((1, mid), F32), ((27, mid, out), F32), ((1, out), F32)),
        *mine,
        *other,
        scratch=(((plan.total, LANES), F32),),
    )
    return (features, jnp.swapaxes(one, 1, 2), bias_one.reshape(mid), jnp.swapaxes(two, 1, 2), bias_two.reshape(out))


def solution(mesh):
    in_specs = (P("sample", None, "space"), P(("sample", "space"), None, None), P(), P(), P(), P())
    out_specs = (P(("sample", "space"), None, None), P(), P(), P(), P())
    return jax.shard_map(
        on_device, mesh=mesh, in_specs=in_specs, out_specs=out_specs, check_vma=False
    )
```

```python
import functools
import math

import jax
import jax.numpy as jnp
from jax import lax
from jax.experimental import pallas as pl
from jax.experimental.pallas import tpu as pltpu
from jax.sharding import PartitionSpec as P

SIDE = 8
LEAK_SLOPE = 0.3
LANES = 128
ROWS = 16
SMALL_LIMIT = 4 * 1024 * 1024
BF16 = jnp.bfloat16
F32 = jnp.float32


def gray(number):
    return number ^ (number >> 1)


def odd(number):
    for shift in (8, 4, 2, 1):
        number = number ^ (number >> shift)
    return number & 1


def half_of(plan, sample):
    return (sample % plan.cores) ^ odd(sample // plan.cores)


def own_half(plan):
    return half_of(plan, lax.axis_index("sample"))


def place_in(plan, half):
    group, space = lax.axis_index("sample") // plan.cores, lax.axis_index("space")
    return jnp.where(half == 0, group, space) if plan.crossed else group


def vmem():
    return pl.BlockSpec(memory_space=pltpu.VMEM)


def lane_iota(rows):
    return lax.broadcasted_iota(jnp.int32, (rows, LANES), 1)


def turn(block, shift):
    return pltpu.roll(block, (-shift) % LANES, 1) if shift % LANES else block


def dot(left, right):
    return jnp.dot(left, right, preferred_element_type=F32)


def dot_lanes(left, right):
    return lax.dot_general(left, right, (((1,), (1,)), ((), ())), preferred_element_type=F32)


def in_plane(side, tap):
    high, wide = tap // 3 - 1, tap % 3 - 1
    lane = lane_iota(1)
    row, col = lane // side % side + high, lane % side + wide
    valid = (row >= 0) & (row < side) & (col >= 0) & (col < side)
    return valid, high * side + wide


def weights_kernel(first_ref, second_ref, bias_one_ref, bias_two_ref, conv_one_ref, conv_two_ref, back_ref, col_one_ref, col_two_ref):
    mid, out = first_ref.shape[2], second_ref.shape[2]
    inner, deep = first_ref.shape[1], second_ref.shape[1]

    def eye(size):
        row = lax.broadcasted_iota(jnp.int32, (size, size), 0)
        return row == lax.broadcasted_iota(jnp.int32, (size, size), 1)

    for a in range(3):
        taps = first_ref[9 * a : 9 * a + 9].reshape(9 * inner, mid)
        conv_one_ref[a * mid : (a + 1) * mid, :] = dot_lanes(eye(mid).astype(BF16), taps).astype(BF16)
        taps = second_ref[9 * a : 9 * a + 9].reshape(9 * deep, out)
        conv_two_ref[a * out : (a + 1) * out, :] = dot_lanes(eye(out).astype(BF16), taps).astype(BF16)
        for t in range(9):
            back_ref[a * deep : (a + 1) * deep, t * out : (t + 1) * out] = second_ref[9 * a + t]
    for row_ref, col_ref, size in ((bias_one_ref, col_one_ref, mid), (bias_two_ref, col_two_ref, out)):
        col = jnp.sum(jnp.where(eye(size), row_ref[...], 0.0), axis=1, keepdims=True)
        col_ref[...] = jnp.broadcast_to(col, (size, LANES))


def prepare_weights(kernel_first, bias_first, kernel_second, bias_second):
    first, second = jnp.swapaxes(kernel_first, 1, 2), jnp.swapaxes(kernel_second, 1, 2)
    inner, mid, out = first.shape[1], first.shape[2], second.shape[2]
    shapes = (
        ((3 * mid, 9 * inner), BF16),
        ((3 * out, 9 * mid), BF16),
        ((3 * mid, 9 * out), BF16),
        ((mid, LANES), F32),
        ((out, LANES), F32),
    )
    return pl.pallas_call(
        weights_kernel,
        out_shape=[jax.ShapeDtypeStruct(s, d) for s, d in shapes],
        in_specs=[vmem()] * 4,
        out_specs=[vmem()] * 5,
        compiler_params=pltpu.CompilerParams(vmem_limit_bytes=SMALL_LIMIT),
        name="weights",
    )(first, second, bias_first.reshape(1, -1), bias_second.reshape(1, -1))


def main_kernel(plan, *refs):
    parts, grad_ref, conv_one_ref, conv_two_ref, back_ref, col_one_ref, col_two_ref = (
        refs[: plan.space],
        *refs[plan.space : plan.space + 6],
    )
    feat_ref, keep_ref, send_ref = refs[plan.space + 6 : plan.space + 9]
    x_ref, s_one, t_one, slope_ref, lk_ref, d_one, s_two, t_two, d_two, sd_two, u_two, pay_ref = refs[plan.space + 9 :]
    inner, mid, out = plan.inner, plan.mid, plan.out
    blocks, halves = plan.blocks, plan.halves
    place, own_core = lax.axis_index("space"), own_half(plan)
    side, small = SIDE, SIDE // 2
    plane = side * side
    low = small * small
    lane = lane_iota(1)

    s_one[9 * inner :, :] = jnp.ones((ROWS, blocks * LANES), BF16)
    s_two[9 * mid :, :] = jnp.ones((ROWS, halves * LANES), BF16)
    cell = lax.broadcasted_iota(jnp.int32, (LANES, LANES), 0)
    lanes = lax.broadcasted_iota(jnp.int32, (LANES, LANES), 1)
    parent = (cell % plane // side // 2) * small + cell % side // 2
    pool = jnp.where(parent == lanes % low, 0.125, 0.0).astype(BF16)
    pool = jnp.concatenate([pool, pool], axis=0)
    parent = (lanes % plane // side // 2) * small + lanes % side // 2

    for volume in range(plan.owned):
        for k, part in zip(reversed(range(plan.space)), parts):
            start = (place ^ k) * plan.part_blocks
            for j in range(plan.part_blocks):
                x_ref[start + j] = part[volume, :, j * LANES : (j + 1) * LANES]

        for first_block in range(0, blocks, 8):
            for tap in range(9):
                valid, shift = in_plane(side, tap)
                for j in range(first_block, first_block + 8):
                    block = x_ref[j]
                    if shift:
                        block = jnp.where(valid, turn(block, shift), jnp.zeros_like(block))
                    s_one[tap * inner : (tap + 1) * inner, j * LANES : (j + 1) * LANES] = block
            here = slice(first_block * LANES, (first_block + 8) * LANES)
            t_one[:, here] = dot(conv_one_ref[...], s_one[: 9 * inner, here])

        upper = lane >= plane
        for j in range(blocks):
            here = slice(j * LANES, (j + 1) * LANES)
            before, after = slice(here.start - LANES, here.start), slice(here.stop, here.stop + LANES)
            zero = jnp.zeros((mid, LANES), F32)
            up = jnp.where(upper, t_one[:mid, before] if j else zero, t_one[:mid, here])
            down = jnp.where(upper, t_one[2 * mid :, here], t_one[2 * mid :, after] if j < blocks - 1 else zero)
            pre = t_one[mid : 2 * mid, here] + turn(up + down, plane) + col_one_ref[...]
            slope = jnp.where(pre > 0, 1.0, LEAK_SLOPE)
            slope_ref[:, here] = slope * 0.125
            value = slope * pre
            high = value.astype(BF16)
            lk_ref[j * mid : (j + 1) * mid, :LANES] = high
            lk_ref[j * mid : (j + 1) * mid, LANES:] = (value - high.astype(F32)).astype(BF16)

        means = dot(lk_ref[...], pool)
        for h in range(halves):
            here = slice(h * LANES, (h + 1) * LANES)
            pooled = jnp.zeros((mid, LANES), F32)
            for j in range(LANES // low):
                row = (h * (LANES // low) + j) * mid
                pooled = jnp.where(lane // low == j, means[row : row + mid], pooled)
            pooled = pooled.astype(BF16)
            for tap in range(9):
                valid, shift = in_plane(small, tap)
                block = jnp.where(valid, turn(pooled, shift), jnp.zeros_like(pooled)) if shift else pooled
                s_two[tap * mid : (tap + 1) * mid, here] = block

        t_two[...] = dot(conv_two_ref[...], s_two[: 9 * mid, :])
        deltas = []
        for h in range(halves):
            here = slice(h * LANES, (h + 1) * LANES)
            before, after = slice(here.start - LANES, here.start), slice(here.stop, here.stop + LANES)
            zero = jnp.zeros((out, LANES), F32)
            up = jnp.where(lane >= LANES - low, t_two[:out, before] if h else zero, t_two[:out, here])
            down = jnp.where(lane < low, t_two[2 * out :, after] if h < halves - 1 else zero, t_two[2 * out :, here])
            pre = t_two[out : 2 * out, here] + turn(up, -low) + turn(down, low) + col_two_ref[...]
            slope = jnp.where(pre > 0, 1.0, LEAK_SLOPE)
            feat_ref[volume, :, here] = (slope * pre).astype(BF16)
            delta = (grad_ref[volume, :, here].astype(F32) * slope).astype(BF16)
            deltas.append(delta)
            for tap in range(9):
                valid, shift = in_plane(small, 8 - tap)
                block = jnp.where(valid, turn(delta, shift), jnp.zeros_like(delta)) if shift else delta
                sd_two[tap * out : (tap + 1) * out, here] = block

        for h in range(halves):
            here = slice(h * LANES, (h + 1) * LANES)
            zero = jnp.zeros((out, LANES), BF16)
            after = deltas[h + 1] if h < halves - 1 else zero
            before = deltas[h - 1] if h else zero
            d_two[:out, here] = turn(jnp.where(lane < low, after, deltas[h]), low)
            d_two[out : 2 * out, here] = deltas[h]
            d_two[2 * out :, here] = turn(jnp.where(lane >= LANES - low, before, deltas[h]), -low)

        u_two[...] = dot(back_ref[...], sd_two[...])
        spreads = []
        for h in range(halves):
            here = slice(h * LANES, (h + 1) * LANES)
            before, after = slice(here.start - LANES, here.start), slice(here.stop, here.stop + LANES)
            zero = jnp.zeros((mid, LANES), F32)
            down = jnp.where(lane < low, u_two[:mid, after] if h < halves - 1 else zero, u_two[:mid, here])
            up = jnp.where(lane >= LANES - low, u_two[2 * mid :, before] if h else zero, u_two[2 * mid :, here])
            spreads.append((u_two[mid : 2 * mid, here] + turn(down, low) + turn(up, -low)).astype(BF16))
        spread = jnp.concatenate(spreads, axis=0)

        deltas = []
        for j in range(LANES // low):
            unpool = jnp.where(parent + j * low == cell, 1.0, 0.0).astype(BF16)
            deltas.append(dot(spread, unpool))
        wide = []
        for j in range(blocks):
            here = slice(j * LANES, (j + 1) * LANES)
            h, i = j // (LANES // low), j % (LANES // low)
            wide.append(deltas[i][h * mid : (h + 1) * mid] * slope_ref[:, here])
        for j in range(blocks):
            here = slice(j * LANES, (j + 1) * LANES)
            zero = jnp.zeros((mid, LANES), F32)
            after = wide[j + 1] if j < blocks - 1 else zero
            before = wide[j - 1] if j else zero
            d_one[:mid, here] = turn(jnp.where(upper, wide[j], after), plane).astype(BF16)
            d_one[mid : 2 * mid, here] = wide[j].astype(BF16)
            d_one[2 * mid :, here] = turn(jnp.where(upper, before, wide[j]), plane).astype(BF16)

        two = dot_lanes(s_two[...], d_two[...]) * plan.scale_two
        one = dot_lanes(s_one[...], d_one[...]) * plan.scale_one
        first = 9 * inner
        total = 27 * mid
        half = first // 2
        pieces = [(a * 9 * mid, two[: 9 * mid, a * out : (a + 1) * out]) for a in range(3)]
        pieces.append((total, one[:first, : 2 * mid]))
        pieces.append((total + first, jnp.concatenate([one[:half, 2 * mid :], one[half:first, 2 * mid :]], axis=1)))
        row = lax.broadcasted_iota(jnp.int32, (ROWS // 2, LANES), 0)
        own = one[first : first + ROWS // 2, : 2 * mid]
        own = jnp.where(lane_iota(1) < mid, turn(own, mid), 0.0)
        tail = jnp.where(row == 0, two[9 * mid : 9 * mid + ROWS // 2, out : 2 * out], jnp.where(row == 1, own, 0.0))
        if volume:
            tail = tail + pay_ref[plan.total - ROWS : plan.total - ROWS // 2] + pay_ref[plan.total - ROWS // 2 :]
        for start, piece in pieces:
            span = slice(start, start + piece.shape[0])
            pay_ref[span, :] = piece + pay_ref[span, :] if volume else piece
        used = total + first + half
        if not volume and used < plan.total - ROWS:
            pay_ref[used : plan.total - ROWS, :] = jnp.zeros((plan.total - ROWS - used, LANES), F32)
        high = tail.astype(BF16).astype(F32)
        pay_ref[plan.total - ROWS :, :] = jnp.concatenate([high, tail - high], axis=0)

    share = plan.total // plan.cores
    keep_ref[...] = pay_ref[pl.ds(pl.multiple_of(own_core * share, ROWS), share), :]
    send_ref[...] = pay_ref[pl.ds(pl.multiple_of((1 - own_core) * share, ROWS), share), :].astype(BF16)


def split_again(values, plan, last):
    rows = values.shape[0]
    tail = values[rows - ROWS : rows - ROWS // 2] + values[rows - ROWS // 2 :]
    high = tail.astype(BF16).astype(F32)
    parted = jnp.concatenate([high, tail - high], axis=0)
    return jnp.where(last, parted, values[rows - ROWS :])


def core_sum_kernel(plan, keep_ref, got_ref, own_ref, *rest):
    sends, sum_ref = rest[:-1], rest[-1]
    half = own_half(plan)
    place = place_in(plan, half)
    rows = keep_ref.shape[0]
    sum_ref[...] = keep_ref[...] + got_ref[...].astype(F32)
    sum_ref[rows - ROWS :, :] = split_again(sum_ref[rows - ROWS :, :], plan, half == plan.cores - 1)

    def chunk(k):
        return sum_ref[pl.ds(pl.multiple_of((place ^ k) * plan.chunk, ROWS), plan.chunk), :]

    own_ref[...] = chunk(0)
    for k, send in enumerate(sends, start=1):
        send[...] = chunk(k).astype(BF16)


def last_chunk(plan):
    half = own_half(plan)
    return (half == plan.cores - 1) & (place_in(plan, half) == plan.groups - 1)


def group_sum_kernel(plan, own_ref, *rest):
    gots, out_ref = rest[:-1], rest[-1]
    total = own_ref[...]
    for got in gots:
        total = total + got[...].astype(F32)
    rows = total.shape[0]
    out_ref[: rows - ROWS, :] = total[: rows - ROWS].astype(BF16)
    out_ref[rows - ROWS :, :] = split_again(total[rows - ROWS :], plan, last_chunk(plan)).astype(BF16)


def space_sum_kernel(plan, *refs):
    values, out_ref = [ref[...].astype(F32) for ref in refs[:-1]], refs[-1]
    while len(values) > 1:
        values = [values[i] + values[i + 1] for i in range(0, len(values), 2)]
    total = values[0]
    rows = total.shape[0]
    out_ref[: rows - ROWS, :] = total[: rows - ROWS].astype(BF16)
    out_ref[rows - ROWS :, :] = split_again(total[rows - ROWS :], plan, last_chunk(plan)).astype(BF16)


def chunk_in(plan, side, k):
    half = own_half(plan) ^ side
    return half * plan.groups + (place_in(plan, half) ^ k)


def leave_taps(plan, places, refs, held, two_ref, sems):
    rows = plan.chunk
    full, rest = 27 * plan.mid // rows, 27 * plan.mid % rows

    def each(act):
        for i, place in enumerate(places):

            @pl.when(place < full)
            def _(i=i, place=place):
                target = two_ref.at[pl.ds(pl.multiple_of(place * rows, ROWS), rows)]
                act(pltpu.make_async_copy(held.at[i], target, sems.at[i]))

            if rest:

                @pl.when(place == full)
                def _(i=i):
                    target = two_ref.at[full * rows : full * rows + rest]
                    act(pltpu.make_async_copy(held.at[i, :rest], target, sems.at[i]))

    for i, ref in enumerate(refs):
        held[i] = ref[...].astype(F32)
    each(lambda copy: copy.start())
    return lambda: each(lambda copy: copy.wait())


def early_kernel(plan, names, *refs):
    two_ref, held, sems = refs[-3:]
    places = [chunk_in(plan, side, k) for side, k in names]
    leave_taps(plan, places, refs[:-3], held, two_ref, sems)()


def unpack_kernel(plan, names, late, *refs):
    count = len(names)
    chunks, refs = refs[:count], refs[count + 1 :]
    two_ref, one_ref, bias_one_ref, bias_two_ref, held, sums, one_buf, bias_one, bias_two, sems = refs
    inner, mid, out = plan.inner, plan.mid, plan.out
    places = [chunk_in(plan, side, k) for side, k in names]
    finish = leave_taps(plan, places[count - late :], chunks[count - late :], held, two_ref, sems)
    full = 27 * mid // plan.chunk
    for ref, place in zip(chunks, places):

        @pl.when(place >= full)
        def _(ref=ref, place=place):
            start = pl.multiple_of((place - full) * plan.chunk, ROWS)
            sums[pl.ds(start, plan.chunk), :] = ref[...].astype(F32)

    total, first, end = 27 * mid - full * plan.chunk, 9 * inner, plan.total - full * plan.chunk
    copies = []

    def leave(source, target):
        copies.append(pltpu.make_async_copy(source, target, sems.at[late + len(copies)]))
        copies[-1].start()

    pair = sums[total : total + first, :]
    one_buf[0:9] = pair[:, :mid].reshape(9, inner, mid)
    one_buf[9:18] = pair[:, mid:].reshape(9, inner, mid)
    pair = sums[total + first : total + first + first // 2, :]
    pair = jnp.concatenate([pair[:, :mid], pair[:, mid:]], axis=0)
    one_buf[18:27] = pair.reshape(9, inner, mid)
    leave(one_buf, one_ref)
    tail = sums[end - ROWS : end - ROWS // 2, :] + sums[end - ROWS // 2 : end, :]
    bias_two[...] = tail[0:1, :out]
    bias_one[...] = tail[1:2, :mid]
    leave(bias_two, bias_two_ref)
    leave(bias_one, bias_one_ref)
    finish()
    for copy in copies:
        copy.wait()


class Plan:
    def __init__(self, volumes, kernel_first, kernel_second):
        self.space, self.sample = lax.axis_size("space"), lax.axis_size("sample")
        self.inner, self.mid, self.out = kernel_first.shape[2], kernel_first.shape[1], kernel_second.shape[1]
        self.owned = volumes.shape[0] // self.space
        self.part_blocks = volumes.shape[2] // LANES
        self.blocks = self.part_blocks * self.space
        self.halves = self.blocks // 8
        self.cores = 2
        self.groups = self.sample // self.cores
        self.crossed = self.groups == self.space
        cells = self.blocks * LANES * volumes.shape[0] * self.sample
        self.scale_one = 1.0 / math.sqrt(cells)
        self.scale_two = 1.0 / math.sqrt(cells // 8)
        used = 27 * self.mid + 9 * self.inner * 3 // 2 + ROWS
        step = ROWS * self.groups * self.cores
        self.total = -(-used // step) * step
        self.chunk = self.total // self.groups // self.cores


def call(kernel, plan, name, out_shapes, *args, scratch=(), limit=SMALL_LIMIT):
    return pl.pallas_call(
        functools.partial(kernel, plan),
        out_shape=[jax.ShapeDtypeStruct(s, d) for s, d in out_shapes],
        in_specs=[vmem()] * len(args),
        out_specs=[vmem()] * len(out_shapes),
        scratch_shapes=[pltpu.VMEM(s, d) for s, d in scratch],
        compiler_params=pltpu.CompilerParams(vmem_limit_bytes=limit),
        name=name,
    )(*args)


def swap(value, axis, k):
    return lax.ppermute(value, axis, [(i, i ^ k) for i in range(lax.axis_size(axis))])


def trade(plan, value, k, within):
    pairs = []
    for sample in range(plan.sample):
        for space in range(plan.space):
            half = half_of(plan, sample)
            group, other = sample // plan.cores, space
            if (plan.crossed and half == 1) == within:
                other = other ^ k
            else:
                group = group ^ k
            core = half ^ half_of(plan, group * plan.cores)
            pairs.append((sample * plan.space + space, (group * plan.cores + core) * plan.space + other))
    return lax.ppermute(value, ("sample", "space"), pairs)


def on_device(volumes, grad_out, kernel_first, bias_first, kernel_second, bias_second):
    plan = Plan(volumes, kernel_first, kernel_second)
    inner, mid, out = plan.inner, plan.mid, plan.out
    me = lax.axis_index("space")

    def piece(k):
        return lax.dynamic_slice_in_dim(volumes, (me ^ k) * plan.owned, plan.owned, axis=0)

    parts = [piece(0)] + [swap(piece(k), "space", k) for k in range(1, plan.space)]
    weights = prepare_weights(kernel_first, bias_first, kernel_second, bias_second)
    cells, small = plan.blocks * LANES, plan.halves * LANES
    share = plan.total // plan.cores
    scratch = (
        ((plan.blocks, inner, LANES), BF16),
        ((9 * inner + ROWS, cells), BF16),
        ((3 * mid, cells), F32),
        ((mid, cells), F32),
        ((plan.blocks * mid, 2 * LANES), BF16),
        ((3 * mid, cells), BF16),
        ((9 * mid + ROWS, small), BF16),
        ((3 * out, small), F32),
        ((3 * out, small), BF16),
        ((9 * out, small), BF16),
        ((3 * mid, small), F32),
        ((plan.total, LANES), F32),
    )
    features, keep, send = call(
        main_kernel,
        plan,
        "main",
        (((plan.owned, out, small), BF16), ((share, LANES), F32), ((share, LANES), BF16)),
        *reversed(parts),
        grad_out,
        *weights,
        scratch=scratch,
        limit=48 * 1024 * 1024,
    )
    chunk = (plan.chunk, LANES)
    got = swap(send, "sample", 1)
    own, *sends = call(core_sum_kernel, plan, "core_sum", ((chunk, F32),) + ((chunk, BF16),) * (plan.groups - 1), keep, got, scratch=(((share, LANES), F32),))
    gots = [trade(plan, s, k, True) for k, s in enumerate(sends, start=1)]
    (partial,) = call(group_sum_kernel, plan, "group_sum", ((chunk, BF16),), own, *gots[1:], gots[0])
    gots = [trade(plan, partial, gray(k), False) for k in range(1, plan.space)]
    (whole,) = call(space_sum_kernel, plan, "space_sum", ((chunk, BF16),), partial, *gots)
    mine = [whole] + [trade(plan, whole, gray(k), True) for k in range(1, plan.groups)]
    other = [swap(value, "sample", 1) for value in mine]
    order = [gray(k) for k in range(plan.groups)]
    late = plan.groups // 2
    names = [(0, k) for k in order] + [(1, order[0])] + [(1, k) for k in reversed(order[1:])]
    chunks = [*mine, other[0], *reversed(other[1:])]
    soon = len(chunks) - late
    far = pl.BlockSpec(memory_space=pl.ANY)
    early = pl.pallas_call(
        functools.partial(early_kernel, plan, names[:soon]),
        out_shape=jax.ShapeDtypeStruct((27 * mid, out), F32),
        in_specs=[vmem()] * soon,
        out_specs=far,
        scratch_shapes=[pltpu.VMEM((soon, *chunk), F32), pltpu.SemaphoreType.DMA((soon,))],
        compiler_params=pltpu.CompilerParams(vmem_limit_bytes=SMALL_LIMIT),
        name="early",
    )(*chunks[:soon])
    last = plan.total - 27 * mid // plan.chunk * plan.chunk
    two, one, bias_one, bias_two = pl.pallas_call(
        functools.partial(unpack_kernel, plan, names, late),
        out_shape=[jax.ShapeDtypeStruct(s, F32) for s in ((27 * mid, out), (27, inner, mid), (1, mid), (1, out))],
        in_specs=[vmem()] * len(chunks) + [far],
        out_specs=[far] * 4,
        scratch_shapes=[
            pltpu.VMEM((late, *chunk), F32),
            pltpu.VMEM((last, LANES), F32),
            pltpu.VMEM((27, inner, mid), F32),
            pltpu.VMEM((1, mid), F32),
            pltpu.VMEM((1, out), F32),
            pltpu.SemaphoreType.DMA((late + 3,)),
        ],
        input_output_aliases={len(chunks): 0},
        compiler_params=pltpu.CompilerParams(vmem_limit_bytes=SMALL_LIMIT),
        name="unpack",
    )(*chunks, early)
    two = two.reshape(27, mid, out)
    return (features, jnp.swapaxes(one, 1, 2), bias_one.reshape(mid), jnp.swapaxes(two, 1, 2), bias_two.reshape(out))


def solution(mesh):
    in_specs = (P("sample", None, "space"), P(("sample", "space"), None, None), P(), P(), P(), P())
    out_specs = (P(("sample", "space"), None, None), P(), P(), P(), P())
    return jax.shard_map(
        on_device, mesh=mesh, in_specs=in_specs, out_specs=out_specs, check_vma=False
    )
```

```python
import functools
import math

import jax
import jax.numpy as jnp
from jax import lax
from jax.experimental import pallas as pl
from jax.experimental.pallas import tpu as pltpu
from jax.sharding import PartitionSpec as P

SIDE = 8
LEAK_SLOPE = 0.3
LANES = 128
ROWS = 16
SMALL_LIMIT = 4 * 1024 * 1024
BF16 = jnp.bfloat16
F32 = jnp.float32


def gray(number):
    return number ^ (number >> 1)


def odd(number):
    for shift in (8, 4, 2, 1):
        number = number ^ (number >> shift)
    return number & 1


def half_of(plan, sample):
    return (sample % plan.cores) ^ odd(sample // plan.cores)


def own_half(plan):
    return half_of(plan, lax.axis_index("sample"))


def place_in(plan, half):
    group, space = lax.axis_index("sample") // plan.cores, lax.axis_index("space")
    return jnp.where(half == 0, group, space) if plan.crossed else group


def vmem():
    return pl.BlockSpec(memory_space=pltpu.VMEM)


def lane_iota(rows):
    return lax.broadcasted_iota(jnp.int32, (rows, LANES), 1)


def turn(block, shift):
    return pltpu.roll(block, (-shift) % LANES, 1) if shift % LANES else block


def dot(left, right):
    return jnp.dot(left, right, preferred_element_type=F32)


def dot_lanes(left, right):
    return lax.dot_general(left, right, (((1,), (1,)), ((), ())), preferred_element_type=F32)


def in_plane(side, tap):
    high, wide = tap // 3 - 1, tap % 3 - 1
    lane = lane_iota(1)
    row, col = lane // side % side + high, lane % side + wide
    valid = (row >= 0) & (row < side) & (col >= 0) & (col < side)
    return valid, high * side + wide


def weights_kernel(first_ref, second_ref, bias_one_ref, bias_two_ref, conv_one_ref, conv_two_ref, back_ref, col_one_ref, col_two_ref):
    mid, out = first_ref.shape[2], second_ref.shape[2]
    inner, deep = first_ref.shape[1], second_ref.shape[1]

    def eye(size):
        row = lax.broadcasted_iota(jnp.int32, (size, size), 0)
        return row == lax.broadcasted_iota(jnp.int32, (size, size), 1)

    for a in range(3):
        taps = first_ref[9 * a : 9 * a + 9].reshape(9 * inner, mid)
        conv_one_ref[a * mid : (a + 1) * mid, :] = dot_lanes(eye(mid).astype(BF16), taps).astype(BF16)
        taps = second_ref[9 * a : 9 * a + 9].reshape(9 * deep, out)
        conv_two_ref[a * out : (a + 1) * out, :] = dot_lanes(eye(out).astype(BF16), taps).astype(BF16)
        for t in range(9):
            back_ref[a * deep : (a + 1) * deep, t * out : (t + 1) * out] = second_ref[9 * a + t]
    for row_ref, col_ref, size in ((bias_one_ref, col_one_ref, mid), (bias_two_ref, col_two_ref, out)):
        col = jnp.sum(jnp.where(eye(size), row_ref[...], 0.0), axis=1, keepdims=True)
        col_ref[...] = jnp.broadcast_to(col, (size, LANES))


def prepare_weights(kernel_first, bias_first, kernel_second, bias_second):
    first, second = jnp.swapaxes(kernel_first, 1, 2), jnp.swapaxes(kernel_second, 1, 2)
    inner, mid, out = first.shape[1], first.shape[2], second.shape[2]
    shapes = (
        ((3 * mid, 9 * inner), BF16),
        ((3 * out, 9 * mid), BF16),
        ((3 * mid, 9 * out), BF16),
        ((mid, LANES), F32),
        ((out, LANES), F32),
    )
    return pl.pallas_call(
        weights_kernel,
        out_shape=[jax.ShapeDtypeStruct(s, d) for s, d in shapes],
        in_specs=[vmem()] * 4,
        out_specs=[vmem()] * 5,
        compiler_params=pltpu.CompilerParams(vmem_limit_bytes=SMALL_LIMIT),
        name="weights",
    )(first, second, bias_first.reshape(1, -1), bias_second.reshape(1, -1))


def main_kernel(plan, *refs):
    parts, grad_ref, conv_one_ref, conv_two_ref, back_ref, col_one_ref, col_two_ref = (
        refs[: plan.space],
        *refs[plan.space : plan.space + 6],
    )
    feat_ref, keep_ref, ahead_ref, send_ref = refs[plan.space + 6 : plan.space + 10]
    x_ref, s_one, t_one, slope_ref, lk_ref, d_one, s_two, t_two, d_two, sd_two, u_two, pay_ref = refs[plan.space + 10 :]
    inner, mid, out = plan.inner, plan.mid, plan.out
    blocks, halves = plan.blocks, plan.halves
    place, own_core = lax.axis_index("space"), own_half(plan)
    side, small = SIDE, SIDE // 2
    plane = side * side
    low = small * small
    lane = lane_iota(1)

    s_one[9 * inner :, :] = jnp.ones((ROWS, blocks * LANES), BF16)
    s_two[9 * mid :, :] = jnp.ones((ROWS, halves * LANES), BF16)
    cell = lax.broadcasted_iota(jnp.int32, (LANES, LANES), 0)
    lanes = lax.broadcasted_iota(jnp.int32, (LANES, LANES), 1)
    parent = (cell % plane // side // 2) * small + cell % side // 2
    pool = jnp.where(parent == lanes % low, 0.125, 0.0).astype(BF16)
    pool = jnp.concatenate([pool, pool], axis=0)
    parent = (lanes % plane // side // 2) * small + lanes % side // 2

    for volume in range(plan.owned):
        for k, part in zip(reversed(range(plan.space)), parts):
            start = (place ^ k) * plan.part_blocks
            for j in range(plan.part_blocks):
                x_ref[start + j] = part[volume, :, j * LANES : (j + 1) * LANES]

        for first_block in range(0, blocks, 8):
            for tap in range(9):
                valid, shift = in_plane(side, tap)
                for j in range(first_block, first_block + 8):
                    block = x_ref[j]
                    if shift:
                        block = jnp.where(valid, turn(block, shift), jnp.zeros_like(block))
                    s_one[tap * inner : (tap + 1) * inner, j * LANES : (j + 1) * LANES] = block
            here = slice(first_block * LANES, (first_block + 8) * LANES)
            t_one[:, here] = dot(conv_one_ref[...], s_one[: 9 * inner, here])

        upper = lane >= plane
        for j in range(blocks):
            here = slice(j * LANES, (j + 1) * LANES)
            before, after = slice(here.start - LANES, here.start), slice(here.stop, here.stop + LANES)
            zero = jnp.zeros((mid, LANES), F32)
            up = jnp.where(upper, t_one[:mid, before] if j else zero, t_one[:mid, here])
            down = jnp.where(upper, t_one[2 * mid :, here], t_one[2 * mid :, after] if j < blocks - 1 else zero)
            pre = t_one[mid : 2 * mid, here] + turn(up + down, plane) + col_one_ref[...]
            slope = jnp.where(pre > 0, 1.0, LEAK_SLOPE)
            slope_ref[:, here] = slope * 0.125
            value = slope * pre
            high = value.astype(BF16)
            lk_ref[j * mid : (j + 1) * mid, :LANES] = high
            lk_ref[j * mid : (j + 1) * mid, LANES:] = (value - high.astype(F32)).astype(BF16)

        means = dot(lk_ref[...], pool)
        for h in range(halves):
            here = slice(h * LANES, (h + 1) * LANES)
            pooled = jnp.zeros((mid, LANES), F32)
            for j in range(LANES // low):
                row = (h * (LANES // low) + j) * mid
                pooled = jnp.where(lane // low == j, means[row : row + mid], pooled)
            pooled = pooled.astype(BF16)
            for tap in range(9):
                valid, shift = in_plane(small, tap)
                block = jnp.where(valid, turn(pooled, shift), jnp.zeros_like(pooled)) if shift else pooled
                s_two[tap * mid : (tap + 1) * mid, here] = block

        t_two[...] = dot(conv_two_ref[...], s_two[: 9 * mid, :])
        deltas = []
        for h in range(halves):
            here = slice(h * LANES, (h + 1) * LANES)
            before, after = slice(here.start - LANES, here.start), slice(here.stop, here.stop + LANES)
            zero = jnp.zeros((out, LANES), F32)
            up = jnp.where(lane >= LANES - low, t_two[:out, before] if h else zero, t_two[:out, here])
            down = jnp.where(lane < low, t_two[2 * out :, after] if h < halves - 1 else zero, t_two[2 * out :, here])
            pre = t_two[out : 2 * out, here] + turn(up, -low) + turn(down, low) + col_two_ref[...]
            slope = jnp.where(pre > 0, 1.0, LEAK_SLOPE)
            feat_ref[volume, :, here] = (slope * pre).astype(BF16)
            delta = (grad_ref[volume, :, here].astype(F32) * slope).astype(BF16)
            deltas.append(delta)
            for tap in range(9):
                valid, shift = in_plane(small, 8 - tap)
                block = jnp.where(valid, turn(delta, shift), jnp.zeros_like(delta)) if shift else delta
                sd_two[tap * out : (tap + 1) * out, here] = block

        for h in range(halves):
            here = slice(h * LANES, (h + 1) * LANES)
            zero = jnp.zeros((out, LANES), BF16)
            after = deltas[h + 1] if h < halves - 1 else zero
            before = deltas[h - 1] if h else zero
            d_two[:out, here] = turn(jnp.where(lane < low, after, deltas[h]), low)
            d_two[out : 2 * out, here] = deltas[h]
            d_two[2 * out :, here] = turn(jnp.where(lane >= LANES - low, before, deltas[h]), -low)

        u_two[...] = dot(back_ref[...], sd_two[...])
        spreads = []
        for h in range(halves):
            here = slice(h * LANES, (h + 1) * LANES)
            before, after = slice(here.start - LANES, here.start), slice(here.stop, here.stop + LANES)
            zero = jnp.zeros((mid, LANES), F32)
            down = jnp.where(lane < low, u_two[:mid, after] if h < halves - 1 else zero, u_two[:mid, here])
            up = jnp.where(lane >= LANES - low, u_two[2 * mid :, before] if h else zero, u_two[2 * mid :, here])
            spreads.append((u_two[mid : 2 * mid, here] + turn(down, low) + turn(up, -low)).astype(BF16))
        spread = jnp.concatenate(spreads, axis=0)

        deltas = []
        for j in range(LANES // low):
            unpool = jnp.where(parent + j * low == cell, 1.0, 0.0).astype(BF16)
            deltas.append(dot(spread, unpool))
        wide = []
        for j in range(blocks):
            here = slice(j * LANES, (j + 1) * LANES)
            h, i = j // (LANES // low), j % (LANES // low)
            wide.append(deltas[i][h * mid : (h + 1) * mid] * slope_ref[:, here])
        for j in range(blocks):
            here = slice(j * LANES, (j + 1) * LANES)
            zero = jnp.zeros((mid, LANES), F32)
            after = wide[j + 1] if j < blocks - 1 else zero
            before = wide[j - 1] if j else zero
            d_one[:mid, here] = turn(jnp.where(upper, wide[j], after), plane).astype(BF16)
            d_one[mid : 2 * mid, here] = wide[j].astype(BF16)
            d_one[2 * mid :, here] = turn(jnp.where(upper, before, wide[j]), plane).astype(BF16)

        two = dot_lanes(s_two[...], d_two[...]) * plan.scale_two
        one = dot_lanes(s_one[...], d_one[...]) * plan.scale_one
        first = 9 * inner
        total = 27 * mid
        half = first // 2
        pieces = [(a * 9 * mid, two[: 9 * mid, a * out : (a + 1) * out]) for a in range(3)]
        pieces.append((total, one[:first, : 2 * mid]))
        pieces.append((total + first, jnp.concatenate([one[:half, 2 * mid :], one[half:first, 2 * mid :]], axis=1)))
        row = lax.broadcasted_iota(jnp.int32, (ROWS // 2, LANES), 0)
        own = one[first : first + ROWS // 2, : 2 * mid]
        own = jnp.where(lane_iota(1) < mid, turn(own, mid), 0.0)
        tail = jnp.where(row == 0, two[9 * mid : 9 * mid + ROWS // 2, out : 2 * out], jnp.where(row == 1, own, 0.0))
        if volume:
            tail = tail + pay_ref[plan.total - ROWS : plan.total - ROWS // 2] + pay_ref[plan.total - ROWS // 2 :]
        for start, piece in pieces:
            span = slice(start, start + piece.shape[0])
            pay_ref[span, :] = piece + pay_ref[span, :] if volume else piece
        used = total + first + half
        if not volume and used < plan.total - ROWS:
            pay_ref[used : plan.total - ROWS, :] = jnp.zeros((plan.total - ROWS - used, LANES), F32)
        high = tail.astype(BF16).astype(F32)
        pay_ref[plan.total - ROWS :, :] = jnp.concatenate([high, tail - high], axis=0)

    share = plan.total // plan.cores
    keep_ref[...] = pay_ref[pl.ds(pl.multiple_of(own_core * share, ROWS), share), :]
    there = place_in(plan, 1 - own_core)
    for i, k in enumerate(plan.steps):
        start = (1 - own_core) * share + (there ^ k) * plan.chunk
        value = pay_ref[pl.ds(pl.multiple_of(start, ROWS), plan.chunk), :].astype(BF16)
        if k:
            ahead_ref[i * plan.chunk : (i + 1) * plan.chunk, :] = value
        else:
            send_ref[...] = value


def split_again(values, plan, last):
    rows = values.shape[0]
    tail = values[rows - ROWS : rows - ROWS // 2] + values[rows - ROWS // 2 :]
    high = tail.astype(BF16).astype(F32)
    parted = jnp.concatenate([high, tail - high], axis=0)
    return jnp.where(last, parted, values[rows - ROWS :])


def core_sum_kernel(plan, steps, keep_ref, got_ref, *outs):
    half = own_half(plan)
    place = place_in(plan, half)
    rows = plan.chunk
    for i, (k, out_ref) in enumerate(zip(steps, outs)):
        there = place ^ k
        mine = keep_ref[pl.ds(pl.multiple_of(there * rows, ROWS), rows), :]
        total = mine + got_ref[i * rows : (i + 1) * rows, :].astype(F32)
        last = (half == plan.cores - 1) & (there == plan.groups - 1)
        out_ref[: rows - ROWS, :] = total[: rows - ROWS].astype(out_ref.dtype)
        out_ref[rows - ROWS :, :] = split_again(total[rows - ROWS :], plan, last).astype(out_ref.dtype)


def last_chunk(plan):
    half = own_half(plan)
    return (half == plan.cores - 1) & (place_in(plan, half) == plan.groups - 1)


def group_sum_kernel(plan, own_ref, *rest):
    gots, out_ref = rest[:-1], rest[-1]
    total = own_ref[...]
    for got in gots:
        total = total + got[...].astype(F32)
    rows = total.shape[0]
    out_ref[: rows - ROWS, :] = total[: rows - ROWS].astype(BF16)
    out_ref[rows - ROWS :, :] = split_again(total[rows - ROWS :], plan, last_chunk(plan)).astype(BF16)


def space_sum_kernel(plan, *refs):
    values, out_ref = [ref[...].astype(F32) for ref in refs[:-1]], refs[-1]
    while len(values) > 1:
        values = [values[i] + values[i + 1] for i in range(0, len(values), 2)]
    total = values[0]
    rows = total.shape[0]
    out_ref[: rows - ROWS, :] = total[: rows - ROWS].astype(BF16)
    out_ref[rows - ROWS :, :] = split_again(total[rows - ROWS :], plan, last_chunk(plan)).astype(BF16)


def chunk_in(plan, side, k):
    half = own_half(plan) ^ side
    return half * plan.groups + (place_in(plan, half) ^ k)


def leave_taps(plan, places, refs, held, two_ref, sems):
    rows = plan.chunk
    full, rest = 27 * plan.mid // rows, 27 * plan.mid % rows

    def each(act):
        for i, place in enumerate(places):

            @pl.when(place < full)
            def _(i=i, place=place):
                target = two_ref.at[pl.ds(pl.multiple_of(place * rows, ROWS), rows)]
                act(pltpu.make_async_copy(held.at[i], target, sems.at[i]))

            if rest:

                @pl.when(place == full)
                def _(i=i):
                    target = two_ref.at[full * rows : full * rows + rest]
                    act(pltpu.make_async_copy(held.at[i, :rest], target, sems.at[i]))

    for i, ref in enumerate(refs):
        held[i] = ref[...].astype(F32)
    each(lambda copy: copy.start())
    return lambda: each(lambda copy: copy.wait())


def early_kernel(plan, names, *refs):
    two_ref, held, sems = refs[-3:]
    places = [chunk_in(plan, side, k) for side, k in names]
    leave_taps(plan, places, refs[:-3], held, two_ref, sems)()


def unpack_kernel(plan, names, late, *refs):
    count = len(names)
    chunks, refs = refs[:count], refs[count + 1 :]
    two_ref, one_ref, bias_one_ref, bias_two_ref, held, sums, one_buf, bias_one, bias_two, sems = refs
    inner, mid, out = plan.inner, plan.mid, plan.out
    places = [chunk_in(plan, side, k) for side, k in names]
    finish = leave_taps(plan, places[count - late :], chunks[count - late :], held, two_ref, sems)
    full = 27 * mid // plan.chunk
    for ref, place in zip(chunks, places):

        @pl.when(place >= full)
        def _(ref=ref, place=place):
            start = pl.multiple_of((place - full) * plan.chunk, ROWS)
            sums[pl.ds(start, plan.chunk), :] = ref[...].astype(F32)

    total, first, end = 27 * mid - full * plan.chunk, 9 * inner, plan.total - full * plan.chunk
    copies = []

    def leave(source, target):
        copies.append(pltpu.make_async_copy(source, target, sems.at[late + len(copies)]))
        copies[-1].start()

    pair = sums[total : total + first, :]
    one_buf[0:9] = pair[:, :mid].reshape(9, inner, mid)
    one_buf[9:18] = pair[:, mid:].reshape(9, inner, mid)
    pair = sums[total + first : total + first + first // 2, :]
    pair = jnp.concatenate([pair[:, :mid], pair[:, mid:]], axis=0)
    one_buf[18:27] = pair.reshape(9, inner, mid)
    leave(one_buf, one_ref)
    tail = sums[end - ROWS : end - ROWS // 2, :] + sums[end - ROWS // 2 : end, :]
    bias_two[...] = tail[0:1, :out]
    bias_one[...] = tail[1:2, :mid]
    leave(bias_two, bias_two_ref)
    leave(bias_one, bias_one_ref)
    finish()
    for copy in copies:
        copy.wait()


class Plan:
    def __init__(self, volumes, kernel_first, kernel_second):
        self.space, self.sample = lax.axis_size("space"), lax.axis_size("sample")
        self.inner, self.mid, self.out = kernel_first.shape[2], kernel_first.shape[1], kernel_second.shape[1]
        self.owned = volumes.shape[0] // self.space
        self.part_blocks = volumes.shape[2] // LANES
        self.blocks = self.part_blocks * self.space
        self.halves = self.blocks // 8
        self.cores = 2
        self.groups = self.sample // self.cores
        self.steps = [*range(1, self.groups), 0]
        self.crossed = self.groups == self.space
        cells = self.blocks * LANES * volumes.shape[0] * self.sample
        self.scale_one = 1.0 / math.sqrt(cells)
        self.scale_two = 1.0 / math.sqrt(cells // 8)
        used = 27 * self.mid + 9 * self.inner * 3 // 2 + ROWS
        step = ROWS * self.groups * self.cores
        self.total = -(-used // step) * step
        self.chunk = self.total // self.groups // self.cores


def call(kernel, plan, name, out_shapes, *args, scratch=(), limit=SMALL_LIMIT):
    return pl.pallas_call(
        functools.partial(kernel, plan),
        out_shape=[jax.ShapeDtypeStruct(s, d) for s, d in out_shapes],
        in_specs=[vmem()] * len(args),
        out_specs=[vmem()] * len(out_shapes),
        scratch_shapes=[pltpu.VMEM(s, d) for s, d in scratch],
        compiler_params=pltpu.CompilerParams(vmem_limit_bytes=limit),
        name=name,
    )(*args)


def swap(value, axis, k):
    return lax.ppermute(value, axis, [(i, i ^ k) for i in range(lax.axis_size(axis))])


def trade(plan, value, k, within):
    pairs = []
    for sample in range(plan.sample):
        for space in range(plan.space):
            half = half_of(plan, sample)
            group, other = sample // plan.cores, space
            if (plan.crossed and half == 1) == within:
                other = other ^ k
            else:
                group = group ^ k
            core = half ^ half_of(plan, group * plan.cores)
            pairs.append((sample * plan.space + space, (group * plan.cores + core) * plan.space + other))
    return lax.ppermute(value, ("sample", "space"), pairs)


def on_device(volumes, grad_out, kernel_first, bias_first, kernel_second, bias_second):
    plan = Plan(volumes, kernel_first, kernel_second)
    inner, mid, out = plan.inner, plan.mid, plan.out
    me = lax.axis_index("space")

    def piece(k):
        return lax.dynamic_slice_in_dim(volumes, (me ^ k) * plan.owned, plan.owned, axis=0)

    parts = [piece(0)] + [swap(piece(k), "space", k) for k in range(1, plan.space)]
    weights = prepare_weights(kernel_first, bias_first, kernel_second, bias_second)
    cells, small = plan.blocks * LANES, plan.halves * LANES
    share = plan.total // plan.cores
    scratch = (
        ((plan.blocks, inner, LANES), BF16),
        ((9 * inner + ROWS, cells), BF16),
        ((3 * mid, cells), F32),
        ((mid, cells), F32),
        ((plan.blocks * mid, 2 * LANES), BF16),
        ((3 * mid, cells), BF16),
        ((9 * mid + ROWS, small), BF16),
        ((3 * out, small), F32),
        ((3 * out, small), BF16),
        ((9 * out, small), BF16),
        ((3 * mid, small), F32),
        ((plan.total, LANES), F32),
    )
    features, keep, ahead, send = call(
        main_kernel,
        plan,
        "main",
        (((plan.owned, out, small), BF16), ((share, LANES), F32), ((share - plan.chunk, LANES), BF16), ((plan.chunk, LANES), BF16)),
        *reversed(parts),
        grad_out,
        *weights,
        scratch=scratch,
        limit=48 * 1024 * 1024,
    )
    chunk = (plan.chunk, LANES)
    got_ahead, got = swap(ahead, "sample", 1), swap(send, "sample", 1)
    steps = plan.steps
    summed = {}
    for part, value in ((steps[:-1], got_ahead), (steps[-1:], got)):
        sums = call(
            lambda plan, *refs, part=part: core_sum_kernel(plan, part, *refs),
            plan,
            "core_sum",
            [(chunk, BF16 if k else F32) for k in part],
            keep,
            value,
        )
        summed.update(zip(part, sums))
    own, sends = summed[0], [summed[k] for k in range(1, plan.groups)]
    gots = [trade(plan, s, k, True) for k, s in enumerate(sends, start=1)]
    (partial,) = call(group_sum_kernel, plan, "group_sum", ((chunk, BF16),), own, *gots[1:], gots[0])
    gots = [trade(plan, partial, gray(k), False) for k in range(1, plan.space)]
    (whole,) = call(space_sum_kernel, plan, "space_sum", ((chunk, BF16),), partial, *gots)
    mine = [whole] + [trade(plan, whole, gray(k), True) for k in range(1, plan.groups)]
    other = [swap(value, "sample", 1) for value in mine]
    order = [gray(k) for k in range(plan.groups)]
    late = plan.groups // 2
    names = [(0, k) for k in order] + [(1, order[0])] + [(1, k) for k in reversed(order[1:])]
    chunks = [*mine, other[0], *reversed(other[1:])]
    soon = len(chunks) - late
    far = pl.BlockSpec(memory_space=pl.ANY)
    early = pl.pallas_call(
        functools.partial(early_kernel, plan, names[:soon]),
        out_shape=jax.ShapeDtypeStruct((27 * mid, out), F32),
        in_specs=[vmem()] * soon,
        out_specs=far,
        scratch_shapes=[pltpu.VMEM((soon, *chunk), F32), pltpu.SemaphoreType.DMA((soon,))],
        compiler_params=pltpu.CompilerParams(vmem_limit_bytes=SMALL_LIMIT),
        name="early",
    )(*chunks[:soon])
    last = plan.total - 27 * mid // plan.chunk * plan.chunk
    two, one, bias_one, bias_two = pl.pallas_call(
        functools.partial(unpack_kernel, plan, names, late),
        out_shape=[jax.ShapeDtypeStruct(s, F32) for s in ((27 * mid, out), (27, inner, mid), (1, mid), (1, out))],
        in_specs=[vmem()] * len(chunks) + [far],
        out_specs=[far] * 4,
        scratch_shapes=[
            pltpu.VMEM((late, *chunk), F32),
            pltpu.VMEM((last, LANES), F32),
            pltpu.VMEM((27, inner, mid), F32),
            pltpu.VMEM((1, mid), F32),
            pltpu.VMEM((1, out), F32),
            pltpu.SemaphoreType.DMA((late + 3,)),
        ],
        input_output_aliases={len(chunks): 0},
        compiler_params=pltpu.CompilerParams(vmem_limit_bytes=SMALL_LIMIT),
        name="unpack",
    )(*chunks, early)
    two = two.reshape(27, mid, out)
    return (features, jnp.swapaxes(one, 1, 2), bias_one.reshape(mid), jnp.swapaxes(two, 1, 2), bias_two.reshape(out))


def solution(mesh):
    in_specs = (P("sample", None, "space"), P(("sample", "space"), None, None), P(), P(), P(), P())
    out_specs = (P(("sample", "space"), None, None), P(), P(), P(), P())
    return jax.shard_map(
        on_device, mesh=mesh, in_specs=in_specs, out_specs=out_specs, check_vma=False
    )
```
